256 devices in a mesh: dp: 16 (over y, z_hi, core), seq: 16 (over x, z_lo).
Axes of the slice: x: 4, y: 4, z: 8 (z_hi: 2, z_lo: 4; z = z_hi * 4 + z_lo), core: 2. Of those that a mesh axis runs over, the one named last changes fastest.
Arguments:
- queries: bfloat16 [16, 2048, 4096], P('dp', 'seq'), may hold values from -8 to 8
- key_vectors: bfloat16 [16, 2048, 4096], P('dp', 'seq'), may hold values from -8 to 8
- value_vectors: bfloat16 [16, 2048, 4096], P('dp', 'seq'), may hold values from -6 to 6
- cotangent: bfloat16 [16, 2048, 4096], P('dp', 'seq'), may hold values from -6 to 6
- conv_weight: float32 [32, 9], P('seq'), may hold values from -1 to 1
Outputs:
- query_grad: bfloat16 [16, 2048, 4096], P('dp', 'seq')
- key_grad: bfloat16 [16, 2048, 4096], P('dp', 'seq')
- value_grad: bfloat16 [16, 2048, 4096], P('dp', 'seq')
- conv_grad: float32 [32, 9], P('seq')
The draws below stay inside these ranges and needn't reach their ends.
All inputs are finite; a program needn't handle non-finite values.
Results may differ from the reference program's by a relative error of at most 0.018.
The reference program's roundings to bfloat16 on the way (of `mixed`) count: a program that leaves them out, or rounds other values in their place, can miss the bound.
Values may be sent and summed in bfloat16 or wider, within the bound.
A program may use at most 128 MiB of HBM per device.

```python
import jax
import jax.numpy as jnp
from jax import lax

D = 4096
HEADS = 32
HD = 128
LANDMARKS = 128
KW = 9
ITERS = 6
REPLICAS = 16
SEQLEN = 2048
SEG = 16


def normal_field(key):
    seg_key, tok_key = jax.random.split(key, 2)
    seg_part = jnp.clip(jax.random.normal(seg_key, (REPLICAS, LANDMARKS, D), jnp.float32), -3.0, 3.0)
    tok_part = jnp.clip(jax.random.normal(tok_key, (REPLICAS, SEQLEN, D), jnp.float32), -3.0, 3.0)
    return 1.5 * jnp.repeat(seg_part, SEG, axis=1) + 0.7 * tok_part


def draw_queries(key, part):
    key = jax.random.fold_in(key, 7)
    field = normal_field(key)
    return field.astype(jnp.bfloat16)


def draw_key_vectors(key, part):
    key = jax.random.fold_in(key, 8)
    field = normal_field(key)
    return field.astype(jnp.bfloat16)


def shard_levels(rng, shape, shards, least, top_value):
    def one(axis_at, shards_of):
        heights = jax.random.uniform(jax.random.fold_in(jax.random.fold_in(rng, 6), axis_at), (shards_of,), jnp.float32, least / len(shards), top_value / len(shards))
        return jnp.repeat(jnp.exp(heights), shape[axis_at] // shards_of).reshape((-1,) + (1,) * (len(shape) - axis_at - 1))

    gain = one(*shards[0])
    for cut in shards[1:]:
        gain = gain * one(*cut)
    return gain


def bell_draw(stream_key, dims, scale, limit, cuts=(), kind=jnp.bfloat16):
    values = jax.random.normal(stream_key, dims, jnp.float32) * scale
    if len(cuts) > 0:
        values = shard_levels(stream_key, dims, cuts, -0.22, 0.18) * values
    return jnp.clip(values, min=-limit, max=limit).astype(kind)


def setup_inputs(seed: int = 0) -> dict:
    splits = jax.random.split(jax.random.key(seed), 6)
    return {
        "queries": draw_queries(jax.random.fold_in(splits[5], 71), 0),
        "key_vectors": draw_key_vectors(jax.random.fold_in(splits[5], 71), 0),
        "value_vectors": bell_draw(splits[2], (REPLICAS, SEQLEN, D), 1.0, 6.0, ((0, 16), (1, 16))),
        "cotangent": bell_draw(splits[3], (REPLICAS, SEQLEN, D), 1.0, 6.0, ((0, 16), (1, 16))),
        "conv_weight": bell_draw(splits[4], (HEADS, KW), 0.2, 1.0, ((0, 16),), jnp.float32),
    }


def kernel_inverse(query_rows, key_rows):
    length = query_rows.shape[0]
    query_marks = lax.optimization_barrier(jnp.mean(query_rows.astype(jnp.float32).reshape(LANDMARKS, length // LANDMARKS, HD), axis=1)).astype(jnp.bfloat16)
    key_marks = lax.optimization_barrier(jnp.mean(key_rows.astype(jnp.float32).reshape(LANDMARKS, length // LANDMARKS, HD), axis=1)).astype(jnp.bfloat16)
    middle = jax.nn.softmax(jnp.dot(query_marks, key_marks.T, preferred_element_type=jnp.float32) * HD ** (-0.5), axis=-1)
    factor = lax.stop_gradient(1.0 / (jnp.max(lax.optimization_barrier(jnp.sum(middle, axis=0))) * jnp.max(lax.optimization_barrier(jnp.sum(middle, axis=1)))))
    inverse = factor * middle.T
    eye_mat = jnp.eye(LANDMARKS, dtype=middle.dtype)
    for step in range(ITERS):
        product = jnp.dot(middle, inverse, precision=lax.Precision.HIGHEST)
        inner = 7.0 * eye_mat - product
        inner = 15.0 * eye_mat - jnp.dot(product, inner, precision=lax.Precision.HIGHEST)
        inner = 13.0 * eye_mat - jnp.dot(product, inner, precision=lax.Precision.HIGHEST)
        inverse = 0.25 * jnp.dot(inverse, inner, precision=lax.Precision.HIGHEST)
    return (query_marks, key_marks, inverse)

def conv_values(value_rows, taps):
    length = value_rows.shape[0]
    width = taps.shape[0]
    half = width // 2
    padded = jnp.pad(value_rows.astype(jnp.float32), ((half, half), (0, 0)))
    total = jnp.zeros(value_rows.shape, jnp.float32)
    for offset in range(width):
        total = total + taps[offset] * padded[offset:offset + length]
    return total

def attend(query_rows, key_rows, value_rows, taps, query_marks, key_marks, inverse):
    left = jax.nn.softmax(jnp.dot(query_rows, key_marks.T, preferred_element_type=jnp.float32) * HD ** (-0.5), axis=-1).astype(jnp.bfloat16)
    right = jax.nn.softmax(jnp.dot(query_marks, key_rows.T, preferred_element_type=jnp.float32) * HD ** (-0.5), axis=-1).astype(jnp.bfloat16)
    summary = jnp.dot(right, value_rows, preferred_element_type=jnp.float32)
    mixed = jnp.dot(inverse, summary, precision=lax.Precision.HIGHEST).astype(jnp.bfloat16)
    return jnp.dot(left, mixed, preferred_element_type=jnp.float32) + conv_values(value_rows, taps)

def head_gradients(query_rows, key_rows, value_rows, cot_rows, taps):

    def forward(query_in, key_in, value_in, taps_in):
        marks = kernel_inverse(query_in, key_in)
        return attend(query_in, key_in, value_in, taps_in, marks[0], marks[1], marks[2])
    result, pullback = jax.vjp(forward, query_rows, key_rows, value_rows, taps)
    return pullback(cot_rows.astype(jnp.float32))

def reference(queries, key_vectors, value_vectors, cotangent, conv_weight):
    shape_four = (REPLICAS, SEQLEN, HEADS, HD)
    query_four = queries.reshape(shape_four)
    key_four = key_vectors.reshape(shape_four)
    value_four = value_vectors.reshape(shape_four)
    cot_four = cotangent.reshape(shape_four)

    def per_head(head_index):
        taps = lax.dynamic_index_in_dim(conv_weight, head_index, 0, False)

        def per_replica(replica):

            def select(array):
                return lax.dynamic_index_in_dim(lax.dynamic_index_in_dim(array, replica, 0, False), head_index, 1, False)
            return head_gradients(select(query_four), select(key_four), select(value_four), select(cot_four), taps)
        grads = lax.map(per_replica, jnp.arange(REPLICAS, dtype=jnp.int32))
        return (grads[0], grads[1], grads[2], lax.optimization_barrier(jnp.sum(grads[3], axis=0)))
    query_all, key_all, value_all, conv_grad = lax.map(per_head, jnp.arange(HEADS, dtype=jnp.int32))

    def back(array):
        return jnp.transpose(array, (1, 2, 0, 3)).reshape(REPLICAS, SEQLEN, D)
    return (back(query_all), back(key_all), back(value_all), conv_grad)
```

```python
import jax
import jax.numpy as jnp
from jax import lax
from jax.experimental import pallas as pl
from jax.experimental.pallas import tpu as pltpu
from jax.sharding import PartitionSpec as P

HD = 128
LM = 128
ITERS = 6
KW = 9
SEG = 16
SCALE = HD ** (-0.5)
MESH = pl.DeviceIdType.MESH
BF = jnp.bfloat16
F32 = jnp.float32

NST = 2
RUNS = 4
RUN = 256
EXT = RUN + 32
ORDER = (1, 0, 3, 2)


def dot(a, b, ca=1, cb=0):
    return lax.dot_general(a, b, (((ca,), (cb,)), ((), ())), preferred_element_type=F32)


def split(x):
    high = x.astype(BF)
    return high, (x - high.astype(F32)).astype(BF)


def mm3(a, b):
    left = jnp.concatenate([a[0], a[1], a[0]], axis=1)
    right = jnp.concatenate([b[0], b[0], b[1]], axis=0)
    return dot(left, right)


def rounded(x):
    return x.astype(BF).astype(F32)


def kernel(
    q_in, k_in, v_in, g_in, w_in,
    dq_out, dk_out, dv_out, dw_out,
    qk_full, lm_local, lm_all, marks, w_all, taps_mat,
    land, halo, rf, rt, lf, stats, part, part_in, mxds, delta,
    m_save, inv_save, xt_save, p_save, p2_save, j_save, al_save,
    dkq, dkq_in, mid_grad, tg, dq_buf, out_buf, dw_buf, dw_dp,
    s_loc, s_lm, r_lm, s_lmf, r_lmf, s_in, r_in, s_own, s_w, r_w, s_ms, r_ms,
    s_part, r_part, s_halo, r_halo, s_mx, r_mx, s_dl, r_dl, s_dkq, r_dkq, s_tg, r_tg,
    s_out, r_out, s_outl, s_dw, r_dw, s_dp, r_dp,
):
    dp = lax.axis_index("dp")
    seq = lax.axis_index("seq")
    x = seq // 4
    z = seq % 4
    za = z // 2
    zb = z % 2
    other = 1 - za
    group = x * 2 + zb
    ins = (q_in, k_in, v_in, g_in)
    outs = (dq_out, dk_out, dv_out)
    pending = []

    def member(i):
        p = (group + i) % 8
        return p, (p // 2) * 4 + za * 2 + p % 2

    partner = x * 4 + other * 2 + zb
    cross = x * 4 + other * 2 + (1 - zb)

    def dp_peer(b):
        step = 1 << b
        return dp + step - 2 * step * ((dp // step) % 2)

    def remote(src, dst, ss, rs, to, at=None):
        copy = pltpu.make_async_remote_copy(
            src_ref=src, dst_ref=dst, send_sem=ss, recv_sem=rs,
            device_id=(dp if at is None else at, to), device_id_type=MESH,
        )
        copy.start()
        pending.append(copy)
        return copy

    local = []
    for n, ref in enumerate((q_in, k_in)):
        copy = pltpu.make_async_copy(ref.at[0], qk_full.at[n], s_loc.at[n])
        copy.start()
        local.append(copy)
    halo[...] = jnp.zeros_like(halo)
    w_all[...] = jnp.zeros_like(w_all)
    w_all[z, 0:2, 0:KW] = w_in[...]
    barrier = pltpu.get_barrier_semaphore()
    for i in range(1, 8):
        pl.semaphore_signal(barrier, inc=1, device_id=(dp, member(i)[1]), device_id_type=MESH)
    for to in (partner, cross):
        pl.semaphore_signal(barrier, inc=1, device_id=(dp, to), device_id_type=MESH)
    for b in range(4):
        pl.semaphore_signal(barrier, inc=1, device_id=(dp_peer(b), seq), device_id_type=MESH)
    for copy in local:
        copy.wait()
    rows = lax.broadcasted_iota(jnp.int32, (8, 128), 0)
    cols = lax.broadcasted_iota(jnp.int32, (8, 128), 1)
    averager = jnp.where(cols // SEG == rows, 1.0 / SEG, 0.0).astype(BF)
    for c in range(8):
        cut = slice(512 * c, 512 * c + 512)
        lm_local[:, cut] = jnp.concatenate(
            [dot(averager, qk_full[0, :, cut]), dot(averager, qk_full[1, :, cut])], axis=0
        ).astype(BF)
    pl.semaphore_wait(barrier, 13)

    my_cols = pl.ds(pl.multiple_of(group * 512, 512), 512)
    lm_copies = []
    for i in range(1, 8):
        p, to = member(i)
        lm_copies.append(remote(
            lm_local.at[:, pl.ds(pl.multiple_of(p * 512, 512), 512)], lm_all.at[za, group],
            s_lm.at[i - 1], r_lm.at[i - 1], to))
    lm_own = pltpu.make_async_copy(lm_local.at[:, my_cols], lm_all.at[za, group], s_loc.at[2])
    lm_own.start()
    w_copies = [
        remote(w_all.at[z], w_all.at[z], s_w.at[n], r_w.at[n], to)
        for n, to in enumerate((x * 4 + za * 2 + 1 - zb, partner, cross))
    ]
    in_copies = {}
    for st in range(NST):
        for a in ORDER:
            got = []
            spot = land.at[a, st, x, pl.ds(pl.multiple_of(zb * 128, 128), 128)]
            for i in range(1, 8):
                p, to = member(i)
                cut = pl.ds(pl.multiple_of(p * 512 + st * 256, 256), 256)
                got.append(remote(
                    ins[a].at[0, :, cut], spot, s_in.at[st, a, i - 1], r_in.at[st, a, i - 1], to))
            cut = pl.ds(pl.multiple_of(group * 512 + st * 256, 256), 256)
            own = pltpu.make_async_copy(ins[a].at[0, :, cut], spot, s_own.at[st, a])
            own.start()
            in_copies[st, a] = (got, own)

    def arrive(st, a):
        got, own = in_copies[st, a]
        for copy in got:
            copy.wait_recv()
        own.wait()

    for copy in lm_copies:
        copy.wait_recv()
    lm_own.wait()
    lmf = remote(lm_all.at[za], lm_all.at[za], s_lmf, r_lmf, partner)
    for copy in w_copies:
        copy.wait_recv()

    t_at = lax.broadcasted_iota(jnp.int32, (RUN, EXT), 0)
    u_at = lax.broadcasted_iota(jnp.int32, (RUN, EXT), 1)
    for h in range(4):
        taps = w_all[2 * zb + h // 2, h % 2 : h % 2 + 1, :]
        band = jnp.zeros((RUN, EXT), F32)
        for j in range(KW):
            band = jnp.where(t_at + 20 - u_at == j, taps[:, j : j + 1], band)
        high, low = split(band)
        taps_mat[h, 0] = high
        taps_mat[h, 1] = low

    lmf.wait_recv()
    lm_values = lm_all[...].astype(F32)
    for h in range(4):
        piece = lm_values[:, :, :, 128 * h : 128 * h + 128]
        marks[0, h] = piece[:, :, 0:8].reshape(LM, HD).astype(BF)
        marks[1, h] = piece[:, :, 8:16].reshape(LM, HD).astype(BF)

    r_at = lax.broadcasted_iota(jnp.int32, (LM, LM), 0)
    c_at = lax.broadcasted_iota(jnp.int32, (LM, LM), 1)
    eye = jnp.where(r_at == c_at, 1.0, 0.0).astype(F32)
    state = []
    for st in range(NST):
        logits = dot(marks[0, 2 * st + za], marks[1, 2 * st + za], 1, 1) * SCALE
        e = jnp.exp(logits - jnp.max(logits, axis=1, keepdims=True))
        middle = e / jnp.sum(e, axis=1, keepdims=True)
        top = jnp.max(jnp.sum(middle, axis=0, keepdims=True), axis=1, keepdims=True)
        side = jnp.max(jnp.sum(middle, axis=1, keepdims=True), axis=0, keepdims=True)
        al = 1.0 / (top * side)
        m_save[st] = middle
        al_save[st] = jnp.broadcast_to(al, (8, 128))
        x0 = al * middle.T
        state.append([x0, mm3(split(middle), split(x0))])
    for it in range(ITERS):
        for st in range(NST):
            inv, prod = state[st]
            ps = split(prod)
            prod2 = mm3(ps, ps)
            p2s = split(prod2)
            j_mat = 13.0 * eye - 15.0 * prod + mm3(p2s, split(7.0 * eye - prod))
            js = split(j_mat)
            xts = split(inv.T)
            for n in range(2):
                xt_save[st, it, n] = xts[n]
                p_save[st, it, n] = ps[n]
                p2_save[st, it, n] = p2s[n]
                j_save[st, it, n] = js[n]
            new = 0.25 * mm3(split(inv), js)
            if it < ITERS - 1:
                prod = 0.25 * (13.0 * prod - 15.0 * prod2 + mm3(p2s, split(7.0 * prod - prod2)))
            state[st] = [new, prod]
    for st in range(NST):
        inv_save[st] = state[st][0]

    dw_state = {}

    def dw_start():
        dw_buf[z] = dw_buf[4]
        dw_state["z"] = [
            remote(dw_buf.at[4], dw_buf.at[z], s_dw.at[n], r_dw.at[n], to)
            for n, to in enumerate((x * 4 + za * 2 + 1 - zb, partner, cross))
        ]

    def dw_step(b):
        if b == 0:
            for copy in dw_state["z"]:
                copy.wait_recv()
            both = dw_buf[z // 2] + dw_buf[z // 2 + 2]
            dw_dp[0] = jnp.where(z % 2 == 0, both, jnp.concatenate([both[2:8], both[0:2]], axis=0))
        else:
            dw_state["dp"].wait_recv()
            dw_dp[2 * b] = dw_dp[2 * b - 2] + dw_dp[2 * b - 1]
        if b < 4:
            dw_state["dp"] = remote(
                dw_dp.at[2 * b], dw_dp.at[2 * b + 1], s_dp.at[b], r_dp.at[b], seq, at=dp_peer(b))
        else:
            dw_out[...] = dw_dp[8, 0:2, 0:KW]

    dw_buf[4] = jnp.zeros((8, 128), F32)
    lane = lax.broadcasted_iota(jnp.int32, (1, 128), 1)

    for st in range(NST):

        def head(a, j):
            return land[a, st, :, :, 128 * j : 128 * j + 128].reshape(RUNS * RUN, HD)

        last = st == NST - 1
        arrive(st, 1)
        for j in range(2):
            logits = dot(head(1, j), marks[0, 2 * st + j], 1, 1) * SCALE
            m = jnp.max(logits, axis=0, keepdims=True)
            e = jnp.exp(logits - m)
            rf[st, j] = e
            stats[st, za, 2 * j : 2 * j + 1, :] = m
            stats[st, za, 2 * j + 1 : 2 * j + 2, :] = jnp.sum(e, axis=0, keepdims=True)
        ms = remote(stats.at[st, za], stats.at[st, za], s_ms.at[st], r_ms.at[st], partner)
        arrive(st, 0)
        for j in range(2):
            logits = dot(marks[1, 2 * st + j], head(0, j), 1, 1) * SCALE
            e = jnp.exp(logits - jnp.max(logits, axis=0, keepdims=True))
            lf[st, j] = e * (1.0 / jnp.sum(e, axis=0, keepdims=True))
        ms.wait_recv()
        for j in range(2):
            m1 = stats[st, za, 2 * j : 2 * j + 1, :]
            s1 = stats[st, za, 2 * j + 1 : 2 * j + 2, :]
            m2 = stats[st, other, 2 * j : 2 * j + 1, :]
            s2 = stats[st, other, 2 * j + 1 : 2 * j + 2, :]
            m = jnp.maximum(m1, m2)
            e1 = jnp.exp(m1 - m)
            factor = e1 / (s1 * e1 + s2 * jnp.exp(m2 - m))
            value = rf[st, j] * factor
            rf[st, j] = value
            rt[st, j] = value.astype(BF)
        arrive(st, 3)
        for j in range(2):
            part[st, j, 0] = dot(lf[st, j].astype(BF), head(3, j))
        dm_copy = remote(
            part.at[st, other, 0], part_in.at[st, 0], s_part.at[st, 0], r_part.at[st, 0], partner)

        def send_halo(a, n):
            return [
                remote(
                    land.at[a, st, :, pl.ds(start, 16)], halo.at[st, n, side, pl.ds(za, 4)],
                    s_halo.at[st, n, side], r_halo.at[st, n, side], partner)
                for side, start in ((0, RUN - 16), (1, 0))
            ]

        halos = send_halo(3, 0)
        arrive(st, 2)
        for j in range(2):
            part[st, j, 1] = dot(rt[st, j], head(2, j), 0, 0)
        sum_copy = remote(
            part.at[st, other, 1], part_in.at[st, 1], s_part.at[st, 1], r_part.at[st, 1], partner)
        halos += send_halo(2, 1)

        def extended(a, n, r, j):
            cut = slice(128 * j, 128 * j + 128)
            return jnp.concatenate(
                [halo[st, n, 0, r, :, cut], land[a, st, r, :, cut], halo[st, n, 1, r + 1, :, cut]],
                axis=0)

        for copy in halos[:2]:
            copy.wait_recv()
        for j in range(2):
            for r in range(RUNS):
                g_ext = extended(3, 0, r, j)
                conv = dot(taps_mat[2 * st + j, 0], g_ext) + dot(taps_mat[2 * st + j, 1], g_ext)
                out_buf[2, st, r, :, 128 * j : 128 * j + 128] = conv.astype(BF)

        dm_copy.wait_recv()
        sum_copy.wait_recv()
        dmix = rounded(part[st, za, 0] + part_in[st, 0])
        summary = part[st, za, 1] + part_in[st, 1]
        inv = inv_save[st]
        dms = dmix.astype(BF)
        mixed = jnp.dot(inv, summary, precision=lax.Precision.HIGHEST, preferred_element_type=F32)
        inv_t = split(inv.T)
        dsum = dot(jnp.concatenate([inv_t[0], inv_t[1]], axis=1),
                   jnp.concatenate([dms, dms], axis=0))
        mxds[st, za, 0] = mixed.astype(BF)
        mxds[st, za, 1] = dsum.astype(BF)
        row = jnp.sum((dsum * summary).T, axis=0, keepdims=True)
        delta[st, za] = jnp.broadcast_to(row, (8, 128))
        mx_copy = remote(mxds.at[st, za], mxds.at[st, za], s_mx.at[st], r_mx.at[st], partner)
        dl_copy = remote(delta.at[st, za], delta.at[st, za], s_dl.at[st], r_dl.at[st], partner)

        for copy in halos[2:]:
            copy.wait_recv()
        for j in range(2):
            corr = jnp.zeros((RUN, EXT), F32)
            for r in range(RUNS):
                cut = slice(128 * j, 128 * j + 128)
                corr += dot(land[3, st, r, :, cut], extended(2, 1, r, j), 1, 1)
            line = jnp.zeros((1, 128), F32)
            for t in range(KW):
                band = jnp.where(u_at - t_at - 12 == t, corr, 0.0)
                total = jnp.sum(jnp.sum(band, axis=0, keepdims=True), axis=1, keepdims=True)
                line = jnp.where(lane == t, total, line)
            dw_buf[4, 2 * st + j : 2 * st + j + 1, :] = line
        if last:
            dw_start()

        s_t = split(summary.T)
        grad = dot(jnp.concatenate([dms, dms], axis=1), jnp.concatenate([s_t[0], s_t[1]], axis=0))
        middle = m_save[st]
        m_t = split(middle.T)
        d_mid = jnp.zeros((LM, LM), F32)
        for it in reversed(range(ITERS)):
            xt = (xt_save[st, it, 0], xt_save[st, it, 1])
            ps = (p_save[st, it, 0], p_save[st, it, 1])
            p2s = (p2_save[st, it, 0], p2_save[st, it, 1])
            js = (j_save[st, it, 0], j_save[st, it, 1])
            ws = split(grad)
            g_mat = 0.25 * mm3(xt, ws)
            gs = split(g_mat)
            u_mat = 7.0 * g_mat - mm3(gs, ps)
            us = split(u_mat)
            d_p = mm3(us, ps) + mm3(ps, us) - mm3(p2s, gs) - 15.0 * g_mat
            dps = split(d_p)
            d_mid = d_mid + mm3(dps, xt)
            grad = 0.25 * mm3(ws, js) + mm3(m_t, dps)
        d_mid = d_mid + al_save[st, 0:1, :] * grad.T
        d_log = middle * (d_mid - jnp.sum(middle * d_mid, axis=1, keepdims=True)) * SCALE
        d_log = d_log.astype(BF)
        mid_grad[0] = dot(d_log, marks[1, 2 * st + za])
        mid_grad[1] = dot(d_log, marks[0, 2 * st + za], 0, 0)
        if last:
            dw_step(0)

        mx_copy.wait_recv()
        dl_copy.wait_recv()
        for j in range(2):
            mixed = mxds[st, j, 0]
            ds = mxds[st, j, 1]
            q_marks, k_marks = marks[0, 2 * st + j], marks[1, 2 * st + j]
            left = lf[st, j]
            d_left = rounded(dot(mixed, head(3, j), 1, 1))
            prod = left * d_left
            d_left = ((prod - left * jnp.sum(prod, axis=0, keepdims=True)) * SCALE).astype(BF)
            d_right = rounded(dot(head(2, j), ds, 1, 1))
            d_right = (rf[st, j] * (d_right - delta[st, j, 0:1, :]) * SCALE).astype(BF)
            dkq[st, j, 0] = dot(d_right, head(1, j), 0, 0).astype(BF)
            dkq[st, j, 1] = dot(d_left, head(0, j)).astype(BF)
            dq_buf[0, j] = dot(d_left, k_marks, 0, 0).astype(BF)
            dq_buf[1, j] = dot(d_right, q_marks).astype(BF)
        dkq_copy = remote(
            dkq.at[st, other], dkq_in.at[st], s_dkq.at[st], r_dkq.at[st], partner)
        for j in range(2):
            cut = slice(128 * j, 128 * j + 128)
            d_v = rounded(dot(rt[st, j], mxds[st, j, 1])).reshape(RUNS, RUN, HD)
            out_buf[2, st, :, :, cut] = (out_buf[2, st, :, :, cut].astype(F32) + d_v).astype(BF)

        def send_out(a):
            spot = outs[a].at[0, :, pl.ds(pl.multiple_of(group * 512 + st * 256, 256), 256)]
            for i in range(1, 8):
                p, to = member(i)
                remote(
                    out_buf.at[a, st, p // 2, pl.ds(pl.multiple_of((p % 2) * 128, 128), 128)], spot,
                    s_out.at[st, a, i - 1], r_out.at[st, a, i - 1], to)
            copy = pltpu.make_async_copy(
                out_buf.at[a, st, x, pl.ds(pl.multiple_of(zb * 128, 128), 128)], spot,
                s_outl.at[st, a])
            copy.start()
            return copy

        own_out = [send_out(2)]
        if last:
            dw_step(1)
        dkq_copy.wait_recv()
        for n in range(2):
            total = rounded(dkq[st, za, n].astype(F32) + dkq_in[st, n].astype(F32))
            total = rounded(total + rounded(mid_grad[n])) * (1.0 / SEG)
            tg[st, za, n] = total.astype(BF).reshape(2, LM // 2, HD)
        tg_copy = remote(
            tg.at[st, za, :, other], tg.at[st, za, :, other], s_tg.at[st], r_tg.at[st], partner)
        if last:
            dw_step(2)
        tg_copy.wait_recv()
        for n in (1, 0):
            for j in range(2):
                rest = tg[st, j, n, za].astype(F32)
                rest = jnp.broadcast_to(rest[:, None, :], (LM // 2, SEG, HD))
                total = dq_buf[n, j].astype(F32) + rest.reshape(RUNS * RUN, HD)
                out_buf[n, st, :, :, 128 * j : 128 * j + 128] = total.astype(BF).reshape(
                    RUNS, RUN, HD)
            own_out.append(send_out(n))
        pending.extend(own_out)

    dw_step(3)
    dw_step(4)
    for copy in pending:
        if copy.is_remote:
            copy.wait_send()
        else:
            copy.wait()
    for st in range(NST):
        for a in range(3):
            for i in range(7):
                spot = outs[a].at[0, :, pl.ds(0, 256)]
                pltpu.make_async_remote_copy(
                    src_ref=spot, dst_ref=spot, send_sem=s_out.at[st, a, i],
                    recv_sem=r_out.at[st, a, i], device_id=(dp, partner), device_id_type=MESH,
                ).wait_recv()


def shards(queries, key_vectors, value_vectors, cotangent, conv_weight):
    any_spec = pl.BlockSpec(memory_space=pl.ANY)
    vmem_spec = pl.BlockSpec(memory_space=pltpu.VMEM)
    full = jax.ShapeDtypeStruct(queries.shape, BF)
    dma = pltpu.SemaphoreType.DMA
    square = (LM, HD)
    chain = (NST, ITERS, 2) + square
    return pl.pallas_call(
        kernel,
        out_shape=(full, full, full, jax.ShapeDtypeStruct(conv_weight.shape, F32)),
        in_specs=[any_spec] * 4 + [vmem_spec],
        out_specs=(any_spec, any_spec, any_spec, vmem_spec),
        scratch_shapes=[
            pltpu.VMEM((2, 128, 4096), BF),
            pltpu.VMEM((16, 4096), BF),
            pltpu.VMEM((2, 8, 16, 512), BF),
            pltpu.VMEM((2, 4) + square, BF),
            pltpu.VMEM((4, 8, 128), F32),
            pltpu.VMEM((4, 2, RUN, EXT), BF),
            pltpu.VMEM((4, NST, RUNS, RUN, 256), BF),
            pltpu.VMEM((NST, 2, 2, 5, 16, 256), BF),
            pltpu.VMEM((NST, 2, RUNS * RUN, LM), F32),
            pltpu.VMEM((NST, 2, RUNS * RUN, LM), BF),
            pltpu.VMEM((NST, 2, LM, RUNS * RUN), F32),
            pltpu.VMEM((NST, 2, 8, 128), F32),
            pltpu.VMEM((NST, 2, 2) + square, F32),
            pltpu.VMEM((NST, 2) + square, F32),
            pltpu.VMEM((NST, 2, 2) + square, BF),
            pltpu.VMEM((NST, 2, 8, 128), F32),
            pltpu.VMEM((NST,) + square, F32),
            pltpu.VMEM((NST,) + square, F32),
            pltpu.VMEM(chain, BF),
            pltpu.VMEM(chain, BF),
            pltpu.VMEM(chain, BF),
            pltpu.VMEM(chain, BF),
            pltpu.VMEM((NST, 8, 128), F32),
            pltpu.VMEM((NST, 2, 2) + square, BF),
            pltpu.VMEM((NST, 2) + square, BF),
            pltpu.VMEM((2,) + square, F32),
            pltpu.VMEM((NST, 2, 2, 2, LM // 2, HD), BF),
            pltpu.VMEM((2, 2, RUNS * RUN, HD), BF),
            pltpu.VMEM((3, NST, RUNS, RUN, 256), BF),
            pltpu.VMEM((5, 8, 128), F32),
            pltpu.VMEM((9, 8, 128), F32),
            dma((3,)), dma((7,)), dma((7,)), dma, dma,
            dma((NST, 4, 7)), dma((NST, 4, 7)), dma((NST, 4)),
            dma((3,)), dma((3,)), dma((NST,)), dma((NST,)),
            dma((NST, 2)), dma((NST, 2)), dma((NST, 2, 2)), dma((NST, 2, 2)),
            dma((NST,)), dma((NST,)), dma((NST,)), dma((NST,)),
            dma((NST,)), dma((NST,)), dma((NST,)), dma((NST,)),
            dma((NST, 3, 7)), dma((NST, 3, 7)), dma((NST, 3)),
            dma((3,)), dma((3,)), dma((4,)), dma((4,)),
        ],
        compiler_params=pltpu.CompilerParams(
            collective_id=0, has_side_effects=True, vmem_limit_bytes=56 * 2**20
        ),
        cost_estimate=pl.CostEstimate(flops=2 * 10**9, bytes_accessed=7 * 2**20, transcendentals=0),
    )(queries, key_vectors, value_vectors, cotangent, conv_weight)


def solution(mesh):
    return jax.shard_map(
        shards,
        mesh=mesh,
        in_specs=(
            P("dp", "seq", None),
            P("dp", "seq", None),
            P("dp", "seq", None),
            P("dp", "seq", None),
            P("seq", None),
        ),
        out_specs=(
            P("dp", "seq", None),
            P("dp", "seq", None),
            P("dp", "seq", None),
            P("seq", None),
        ),
        check_vma=False,
    )
```

```python
import jax
import jax.numpy as jnp
from jax import lax
from jax.experimental import pallas as pl
from jax.experimental.pallas import tpu as pltpu
from jax.sharding import PartitionSpec as P

HD = 128
LM = 128
ITERS = 6
KW = 9
SEG = 16
SCALE = HD ** (-0.5)
MESH = pl.DeviceIdType.MESH
BF = jnp.bfloat16
F32 = jnp.float32

DP_STEPS = (1, 4, 8)
ROWS = 32
NST = 2
RUNS = 4
RUN = 256
EXT = RUN + 32
ORDER = (1, 0, 3, 2)


def dot(a, b, ca=1, cb=0):
    return lax.dot_general(a, b, (((ca,), (cb,)), ((), ())), preferred_element_type=F32)


def split(x):
    high = x.astype(BF)
    return high, (x - high.astype(F32)).astype(BF)


def mm3(a, b):
    left = jnp.concatenate([a[0], a[1], a[0]], axis=1)
    right = jnp.concatenate([b[0], b[0], b[1]], axis=0)
    return dot(left, right)


def rounded(x):
    return x.astype(BF).astype(F32)


def kernel(
    q_in, k_in, v_in, g_in, w_in,
    dq_out, dk_out, dv_out, lg_in, dw_out,
    qk_full, lm_local, lm_all, marks, w_all, taps_mat,
    land, halo, pack, pack_in, rf, rt, lf, stats, part, part_bf, part_in,
    m_save, inv_save, xt_save, p_save, p2_save, j_save, al_save,
    dkq, dkq_in, mid_grad, lg_out, out_buf, dw_buf, dw_dp,
    s_loc, s_lm, r_lm, s_lmf, r_lmf, s_in, r_in, s_own, s_w, r_w, s_ms, r_ms,
    s_part, r_part, s_halo, r_halo, s_dkq, r_dkq, s_tg, r_tg,
    s_out, r_out, s_outl, s_lgl, s_dw, r_dw, s_dp, r_dp,
):
    dp = lax.axis_index("dp")
    seq = lax.axis_index("seq")
    x = seq // 4
    z = seq % 4
    za = z // 2
    zb = z % 2
    other = 1 - za
    group = x * 2 + zb
    ins = (q_in, k_in, v_in, g_in)
    outs = (dq_out, dk_out, dv_out)
    pending = []

    def member(i):
        p = (group + i) % 8
        return p, (p // 2) * 4 + za * 2 + p % 2

    partner = x * 4 + other * 2 + zb
    cross = x * 4 + other * 2 + (1 - zb)

    def dp_peer(step):
        return dp + step - 2 * step * ((dp // step) % 2)

    def remote(src, dst, ss, rs, to, at=None):
        copy = pltpu.make_async_remote_copy(
            src_ref=src, dst_ref=dst, send_sem=ss, recv_sem=rs,
            device_id=(dp if at is None else at, to), device_id_type=MESH,
        )
        copy.start()
        pending.append(copy)
        return copy

    local = []
    for n, ref in enumerate((q_in, k_in)):
        copy = pltpu.make_async_copy(ref.at[0], qk_full.at[n], s_loc.at[n])
        copy.start()
        local.append(copy)
    w_all[...] = jnp.zeros_like(w_all)
    w_all[z, 0:2, 0:KW] = w_in[...]
    barrier = pltpu.get_barrier_semaphore()
    for i in range(1, 8):
        pl.semaphore_signal(barrier, inc=1, device_id=(dp, member(i)[1]), device_id_type=MESH)
    flip = x * 4 + za * 2 + 1 - zb
    along_z = [(dp, to) for to in (flip, partner, cross)]
    along_z += [(dp_peer(2), to) for to in (seq, flip, partner, cross)]
    for to in along_z[1:]:
        pl.semaphore_signal(barrier, inc=1, device_id=to, device_id_type=MESH)
    for step in DP_STEPS:
        pl.semaphore_signal(barrier, inc=1, device_id=(dp_peer(step), seq), device_id_type=MESH)
    for copy in local:
        copy.wait()
    rows = lax.broadcasted_iota(jnp.int32, (8, 128), 0)
    cols = lax.broadcasted_iota(jnp.int32, (8, 128), 1)
    averager = jnp.where(cols // SEG == rows, 1.0 / SEG, 0.0).astype(BF)
    for c in range(8):
        cut = slice(512 * c, 512 * c + 512)
        lm_local[:, cut] = jnp.concatenate(
            [dot(averager, qk_full[0, :, cut]), dot(averager, qk_full[1, :, cut])], axis=0
        ).astype(BF)
    pl.semaphore_wait(barrier, 16)

    my_cols = pl.ds(pl.multiple_of(group * 512, 512), 512)
    lm_copies = []
    for i in range(1, 8):
        p, to = member(i)
        lm_copies.append(remote(
            lm_local.at[:, pl.ds(pl.multiple_of(p * 512, 512), 512)], lm_all.at[za, group],
            s_lm.at[i - 1], r_lm.at[i - 1], to))
    lm_own = pltpu.make_async_copy(lm_local.at[:, my_cols], lm_all.at[za, group], s_loc.at[2])
    lm_own.start()
    w_copies = [
        remote(w_all.at[z], w_all.at[z], s_w.at[n], r_w.at[n], to)
        for n, to in enumerate((x * 4 + za * 2 + 1 - zb, partner, cross))
    ]
    in_copies = {}

    def issue(st, a):
        if st >= NST:
            return
        got = []
        spot = land.at[a, st, x, pl.ds(pl.multiple_of(zb * 128, 128), 128)]
        for i in range(1, 8):
            p, to = member(i)
            cut = pl.ds(pl.multiple_of(p * 512 + st * 256, 256), 256)
            got.append(remote(
                ins[a].at[0, :, cut], spot, s_in.at[st, a, i - 1], r_in.at[st, a, i - 1], to))
        cut = pl.ds(pl.multiple_of(group * 512 + st * 256, 256), 256)
        own = pltpu.make_async_copy(ins[a].at[0, :, cut], spot, s_own.at[st, a])
        own.start()
        in_copies[st, a] = (got, own)

    issue(0, 1)
    issue(0, 0)

    def arrive(st, a):
        got, own = in_copies[st, a]
        for copy in got:
            copy.wait_recv()
        own.wait()

    for copy in lm_copies:
        copy.wait_recv()
    lm_own.wait()
    lmf = remote(lm_all.at[za], lm_all.at[za], s_lmf, r_lmf, partner)
    issue(0, 3)
    issue(0, 2)
    for copy in w_copies:
        copy.wait_recv()

    t_at = lax.broadcasted_iota(jnp.int32, (RUN, EXT), 0)
    u_at = lax.broadcasted_iota(jnp.int32, (RUN, EXT), 1)
    for h in range(4):
        taps = w_all[2 * zb + h // 2, h % 2 : h % 2 + 1, :]
        band = jnp.zeros((RUN, EXT), F32)
        for j in range(KW):
            band = jnp.where(t_at + 20 - u_at == j, taps[:, j : j + 1], band)
        high, low = split(band)
        taps_mat[h, 0] = high
        taps_mat[h, 1] = low

    lmf.wait_recv()
    lm_values = lm_all[...].astype(F32)
    for h in range(4):
        piece = lm_values[:, :, :, 128 * h : 128 * h + 128]
        marks[0, h] = piece[:, :, 0:8].reshape(LM, HD).astype(BF)
        marks[1, h] = piece[:, :, 8:16].reshape(LM, HD).astype(BF)

    r_at = lax.broadcasted_iota(jnp.int32, (LM, LM), 0)
    c_at = lax.broadcasted_iota(jnp.int32, (LM, LM), 1)
    eye = jnp.where(r_at == c_at, 1.0, 0.0).astype(F32)

    def invert(st):
        state = []
        for h in (2 * st, 2 * st + 1):
            logits = dot(marks[0, h], marks[1, h], 1, 1) * SCALE
            e = jnp.exp(logits - jnp.max(logits, axis=1, keepdims=True))
            middle = e / jnp.sum(e, axis=1, keepdims=True)
            top = jnp.max(jnp.sum(middle, axis=0, keepdims=True), axis=1, keepdims=True)
            side = jnp.max(jnp.sum(middle, axis=1, keepdims=True), axis=0, keepdims=True)
            al = 1.0 / (top * side)
            m_save[h] = middle
            al_save[h] = jnp.broadcast_to(al, (8, 128))
            x0 = al * middle.T
            state.append([x0, mm3(split(middle), split(x0))])
        for it in range(ITERS):
            for j in range(2):
                inv, prod = state[j]
                h = 2 * st + j
                ps = split(prod)
                prod2 = mm3(ps, ps)
                p2s = split(prod2)
                j_mat = 13.0 * eye - 15.0 * prod + mm3(p2s, split(7.0 * eye - prod))
                js = split(j_mat)
                xts = split(inv.T)
                for n in range(2):
                    xt_save[h, it, n] = xts[n]
                    p_save[h, it, n] = ps[n]
                    p2_save[h, it, n] = p2s[n]
                    j_save[h, it, n] = js[n]
                new = 0.25 * mm3(split(inv), js)
                if it < ITERS - 1:
                    prod = 0.25 * (13.0 * prod - 15.0 * prod2 + mm3(p2s, split(7.0 * prod - prod2)))
                state[j] = [new, prod]
        for j in range(2):
            inv_save[2 * st + j] = state[j][0]

    dw_state = {}

    def dw_start():
        place = (dp // 2) % 2 * 4 + z
        dw_buf[place] = dw_buf[8]
        dw_state["z"] = [
            remote(dw_buf.at[8], dw_buf.at[place], s_dw.at[n], r_dw.at[n], to, at=at)
            for n, (at, to) in enumerate(along_z)
        ]

    def dw_step(b):
        if b == 0:
            for copy in dw_state["z"]:
                copy.wait_recv()
            first = dw_buf[z // 2] + dw_buf[z // 2 + 2]
            both = first + (dw_buf[z // 2 + 4] + dw_buf[z // 2 + 6])
            dw_dp[0] = jnp.where(z % 2 == 0, both, jnp.concatenate([both[2:8], both[0:2]], axis=0))
        else:
            dw_state["dp"].wait_recv()
            dw_dp[2 * b] = dw_dp[2 * b - 2] + dw_dp[2 * b - 1]
        if b < 3:
            dw_state["dp"] = remote(
                dw_dp.at[2 * b], dw_dp.at[2 * b + 1], s_dp.at[b], r_dp.at[b], seq,
                at=dp_peer(DP_STEPS[b]))
        else:
            dw_out[...] = dw_dp[6]

    at64, at16 = (lax.broadcasted_iota(jnp.int32, (16, n), 1) for n in (64, 16))
    to64, to16 = (lax.broadcasted_iota(jnp.int32, (16, n), 0) for n in (64, 16))

    def ones_where(cond):
        return jnp.where(cond, 1.0, 0.0).astype(BF)

    pick_first = ones_where(at64 == (to64 // 4) * 16 + to64 % 4)
    pick_final = ones_where(at64 == (to64 // 4) * 16 + 12 + to64 % 4)
    spread = (
        [ones_where((at16 // 4 == r - 1 + za) & (to16 == 12 + at16 % 4)) for r in range(RUNS)],
        [ones_where((at16 // 4 == r + za) & (to16 == at16 % 4)) for r in range(RUNS)],
    )
    dw_buf[8] = jnp.zeros((8, 128), F32)
    lane = lax.broadcasted_iota(jnp.int32, (1, 128), 1)

    out_copies = {(st, a): [] for st in range(NST) for a in range(3)}
    own_out = {}
    lg_copies = {}

    def finish(st):
        for copy in lg_copies[st]:
            copy.wait_recv()
        for a in (2, 1, 0):
            for copy in out_copies[st, a]:
                copy.wait_recv()
            own_out[st, a].wait()
        own_out[st, 3].wait()

    def head(st, a, j):
        return land[a, st, :, :, 128 * j : 128 * j + 128].reshape(RUNS * RUN, HD)

    def send_halo(st):
        first = land[3, st, :, 0:16, :].reshape(RUNS * 16, 256)
        final = land[3, st, :, RUN - 16 : RUN, :].reshape(RUNS * 16, 256)
        pack[st, 0] = dot(pick_final, final).astype(BF)
        pack[st, 1] = dot(pick_first, first).astype(BF)
        return remote(pack.at[st], pack_in.at[st], s_halo.at[st], r_halo.at[st], partner)

    def extended(st, r, j):
        cut = slice(128 * j, 128 * j + 128)
        return jnp.concatenate(
            [halo[st, 0, r, :, cut], land[3, st, r, :, cut], halo[st, 1, r, :, cut]], axis=0)

    sent = {}

    def prepare(st):
        arrive(st, 1)
        for j in range(2):
            logits = dot(head(st, 1, j), marks[0, 2 * st + j], 1, 1) * SCALE
            m = jnp.max(logits, axis=0, keepdims=True)
            e = jnp.exp(logits - m)
            rf[st, j] = e
            stats[st, za, 2 * j : 2 * j + 1, :] = m
            stats[st, za, 2 * j + 1 : 2 * j + 2, :] = jnp.sum(e, axis=0, keepdims=True)
        ms = remote(stats.at[st, za], stats.at[st, za], s_ms.at[st], r_ms.at[st], partner)
        if st == 0:
            for a in ORDER:
                issue(1, a)
        arrive(st, 0)
        for j in range(2):
            logits = dot(marks[1, 2 * st + j], head(st, 0, j), 1, 1) * SCALE
            e = jnp.exp(logits - jnp.max(logits, axis=0, keepdims=True))
            lf[st, j] = e * (1.0 / jnp.sum(e, axis=0, keepdims=True))
        invert(st)
        arrive(st, 3)
        for j in range(2):
            part[st, 0, j] = dot(lf[st, j].astype(BF), head(st, 3, j))
            part_bf[st, 0, j] = part[st, 0, j].astype(BF)
        sent[st, "dm"] = remote(
            part_bf.at[st, 0], part_in.at[st, 0], s_part.at[st, 0], r_part.at[st, 0], partner)
        sent[st, "halo"] = send_halo(st)
        ms.wait_recv()
        for j in range(2):
            m1 = stats[st, za, 2 * j : 2 * j + 1, :]
            s1 = stats[st, za, 2 * j + 1 : 2 * j + 2, :]
            m2 = stats[st, other, 2 * j : 2 * j + 1, :]
            s2 = stats[st, other, 2 * j + 1 : 2 * j + 2, :]
            m = jnp.maximum(m1, m2)
            e1 = jnp.exp(m1 - m)
            factor = e1 / (s1 * e1 + s2 * jnp.exp(m2 - m))
            value = rf[st, j] * factor
            rf[st, j] = value
            rt[st, j] = value.astype(BF)
        arrive(st, 2)
        for j in range(2):
            part[st, 1, j] = dot(rt[st, j], head(st, 2, j), 0, 0)
            part_bf[st, 1, j] = part[st, 1, j].astype(BF)
        sent[st, "sum"] = remote(
            part_bf.at[st, 1], part_in.at[st, 1], s_part.at[st, 1], r_part.at[st, 1], partner)

    def convolve(st):
        sent[st, "halo"].wait_recv()
        for side in range(2):
            packed = pack_in[st, side]
            for r in range(RUNS):
                halo[st, side, r] = dot(spread[side][r], packed).astype(BF)
        for j in range(2):
            for r in range(RUNS):
                g_ext = extended(st, r, j)
                conv = dot(taps_mat[2 * st + j, 0], g_ext) + dot(taps_mat[2 * st + j, 1], g_ext)
                out_buf[2, st, r, :, 128 * j : 128 * j + 128] = conv.astype(BF)

    def taps_grad(st):
        for j in range(2):
            corr = jnp.zeros((RUN, EXT), F32)
            for r in range(RUNS):
                cut = slice(128 * j, 128 * j + 128)
                corr += dot(land[2, st, r, :, cut], extended(st, r, j), 1, 1)
            line = jnp.zeros((1, 128), F32)
            for t in range(KW):
                band = jnp.where(t_at + 20 - u_at == t, corr, 0.0)
                total = jnp.sum(jnp.sum(band, axis=0, keepdims=True), axis=1, keepdims=True)
                line = jnp.where(lane == t, total, line)
            dw_buf[8, 2 * st + j : 2 * st + j + 1, :] = line

    def totals(st, j):
        dms = (part[st, 0, j] + part_in[st, 0, j].astype(F32)).astype(BF)
        return dms, part[st, 1, j] + part_in[st, 1, j].astype(F32)

    def send_out(st, a):
        spot = outs[a].at[0, :, pl.ds(pl.multiple_of(group * 512 + st * 256, 256), 256)]
        for i in range(1, 8):
            p, to = member(i)
            out_copies[st, a].append(remote(
                out_buf.at[a, st, p // 2, pl.ds(pl.multiple_of((p % 2) * 128, 128), 128)], spot,
                s_out.at[st, a, i - 1], r_out.at[st, a, i - 1], to))
        copy = pltpu.make_async_copy(
            out_buf.at[a, st, x, pl.ds(pl.multiple_of(zb * 128, 128), 128)], spot,
            s_outl.at[st, a])
        copy.start()
        own_out[st, a] = copy

    def grads(st):
        sent[st, "dm"].wait_recv()
        sent[st, "sum"].wait_recv()
        mixeds, dsums, deltas = [], [], []
        for j in range(2):
            dms, summary = totals(st, j)
            inv = inv_save[2 * st + j]
            inv_t = split(inv.T)
            mixed = jnp.dot(
                inv, summary, precision=lax.Precision.HIGHEST, preferred_element_type=F32)
            dsum = dot(jnp.concatenate([inv_t[0], inv_t[1]], axis=1),
                       jnp.concatenate([dms, dms], axis=0))
            mixeds.append(mixed.astype(BF))
            dsums.append(dsum.astype(BF))
            deltas.append(jnp.sum((dsum * summary).T, axis=0, keepdims=True))
        for j in range(2):
            cut = slice(128 * j, 128 * j + 128)
            d_v = rounded(dot(rt[st, j], dsums[j])).reshape(RUNS, RUN, HD)
            out_buf[2, st, :, :, cut] = (out_buf[2, st, :, :, cut].astype(F32) + d_v).astype(BF)
        send_out(st, 2)
        for j in range(2):
            cut = slice(128 * j, 128 * j + 128)
            d_right = rounded(dot(head(st, 2, j), dsums[j], 1, 1))
            d_right = (rf[st, j] * (d_right - deltas[j]) * SCALE).astype(BF)
            d_k = dot(d_right, marks[0, 2 * st + j]).astype(BF)
            out_buf[1, st, :, :, cut] = d_k.reshape(RUNS, RUN, HD)
            dkq[st, 0, :, j] = dot(d_right, head(st, 1, j), 0, 0).astype(BF).reshape(
                2, LM // 2, HD)
        for j in range(2):
            cut = slice(128 * j, 128 * j + 128)
            left = lf[st, j]
            d_left = rounded(dot(mixeds[j], head(st, 3, j), 1, 1))
            prod = left * d_left
            d_left = ((prod - left * jnp.sum(prod, axis=0, keepdims=True)) * SCALE).astype(BF)
            d_q = dot(d_left, marks[1, 2 * st + j], 0, 0).astype(BF)
            out_buf[0, st, :, :, cut] = d_q.reshape(RUNS, RUN, HD)
            dkq[st, 1, :, j] = dot(d_left, head(st, 0, j)).astype(BF).reshape(2, LM // 2, HD)
        sent[st, "dkq"] = remote(
            dkq.at[st, :, other], dkq_in.at[st], s_dkq.at[st], r_dkq.at[st], partner)

    def reverse(st):
        chain = []
        for j in range(2):
            dms, summary = totals(st, j)
            s_t = split(summary.T)
            grad = dot(
                jnp.concatenate([dms, dms], axis=1), jnp.concatenate([s_t[0], s_t[1]], axis=0))
            chain.append([grad, jnp.zeros((LM, LM), F32), split(m_save[2 * st + j].T)])
        for it in reversed(range(ITERS)):
            for j in range(2):
                h = 2 * st + j
                grad, d_mid, m_t = chain[j]
                xt = (xt_save[h, it, 0], xt_save[h, it, 1])
                ps = (p_save[h, it, 0], p_save[h, it, 1])
                p2s = (p2_save[h, it, 0], p2_save[h, it, 1])
                js = (j_save[h, it, 0], j_save[h, it, 1])
                ws = split(grad)
                g_mat = 0.25 * mm3(xt, ws)
                gs = split(g_mat)
                u_mat = 7.0 * g_mat - mm3(gs, ps)
                us = split(u_mat)
                d_p = mm3(us, ps) + mm3(ps, us) - mm3(p2s, gs) - 15.0 * g_mat
                dps = split(d_p)
                d_mid = d_mid + mm3(dps, xt)
                grad = 0.25 * mm3(ws, js) + mm3(m_t, dps)
                chain[j] = [grad, d_mid, m_t]
        for j in range(2):
            h = 2 * st + j
            grad, d_mid, m_t = chain[j]
            middle = m_save[h]
            d_mid = d_mid + al_save[h, 0:1, :] * grad.T
            d_log = middle * (d_mid - jnp.sum(middle * d_mid, axis=1, keepdims=True)) * SCALE
            d_log = d_log.astype(BF)
            mid_grad[0, j] = dot(d_log, marks[1, h]).reshape(2, LM // 2, HD)
            mid_grad[1, j] = dot(d_log, marks[0, h], 0, 0).reshape(2, LM // 2, HD)
        sent[st, "dkq"].wait_recv()
        for j in range(2):
            cut = slice(128 * j, 128 * j + 128)
            both = []
            for n in range(2):
                rest = rounded(dkq[st, n, za, j].astype(F32) + dkq_in[st, n, j].astype(F32))
                rest = rounded(rest + rounded(mid_grad[n, j, za])) * (1.0 / SEG)
                both.append(rest.reshape(8, 8, HD))
            lg_out[st, :, :, cut] = jnp.concatenate(both, axis=1).astype(BF)
        lg_copies[st] = []
        spot = pl.ds(pl.multiple_of(group * 512 + st * 256, 256), 256)
        for i in range(1, 8):
            p, to = member(i)
            lg_copies[st].append(remote(
                lg_out.at[st, p], lg_in.at[:, spot], s_tg.at[st, i - 1], r_tg.at[st, i - 1], to))
        own = pltpu.make_async_copy(lg_out.at[st, group], lg_in.at[:, spot], s_lgl.at[st])
        own.start()
        own_out[st, 3] = own

    prepare(0)
    prepare(1)
    convolve(0)
    grads(0)
    convolve(1)
    taps_grad(0)
    taps_grad(1)
    dw_start()
    grads(1)
    for st in range(NST):
        send_out(st, 1)
        send_out(st, 0)
    dw_step(0)
    reverse(0)
    dw_step(1)
    reverse(1)
    dw_step(2)
    for st in range(NST):
        finish(st)
    dw_step(3)
    for copy in pending:
        copy.wait_send()


def add_marks(dq, dk, dv, marks_grad, dw, dq_out, dk_out, dv_out, dw_out):
    at = (pl.program_id(0) * ROWS + lax.broadcasted_iota(jnp.int32, (ROWS, 16), 0)) // SEG
    col = lax.broadcasted_iota(jnp.int32, (ROWS, 16), 1)
    for n, (part, out) in enumerate(((dq, dq_out), (dk, dk_out))):
        pick = jnp.where(col == at + 8 * n, 1.0, 0.0).astype(BF)
        out[0] = (part[0].astype(F32) + dot(pick, marks_grad[...])).astype(BF)
    dv_out[...] = dv[...]
    dw_out[...] = dw[0:2, 0:KW]


def shards(queries, key_vectors, value_vectors, cotangent, conv_weight):
    any_spec = pl.BlockSpec(memory_space=pl.ANY)
    vmem_spec = pl.BlockSpec(memory_space=pltpu.VMEM)
    full = jax.ShapeDtypeStruct(queries.shape, BF)
    dma = pltpu.SemaphoreType.DMA
    square = (LM, HD)
    chain = (4, ITERS, 2) + square
    dq, dk, dv, marks_grad, dw = pl.pallas_call(
        kernel,
        out_shape=(
            full, full, full, jax.ShapeDtypeStruct((16, full.shape[2]), BF),
            jax.ShapeDtypeStruct((8, 128), F32)),
        in_specs=[any_spec] * 4 + [vmem_spec],
        out_specs=(any_spec,) * 4 + (vmem_spec,),
        scratch_shapes=[
            pltpu.VMEM((2, 128, 4096), BF),
            pltpu.VMEM((16, 4096), BF),
            pltpu.VMEM((2, 8, 16, 512), BF),
            pltpu.VMEM((2, 4) + square, BF),
            pltpu.VMEM((4, 8, 128), F32),
            pltpu.VMEM((4, 2, RUN, EXT), BF),
            pltpu.VMEM((4, NST, RUNS, RUN, 256), BF),
            pltpu.VMEM((NST, 2, RUNS, 16, 256), BF),
            pltpu.VMEM((NST, 2, 16, 256), BF),
            pltpu.VMEM((NST, 2, 16, 256), BF),
            pltpu.VMEM((NST, 2, RUNS * RUN, LM), F32),
            pltpu.VMEM((NST, 2, RUNS * RUN, LM), BF),
            pltpu.VMEM((NST, 2, LM, RUNS * RUN), F32),
            pltpu.VMEM((NST, 2, 8, 128), F32),
            pltpu.VMEM((NST, 2, 2) + square, F32),
            pltpu.VMEM((NST, 2, 2) + square, BF),
            pltpu.VMEM((NST, 2, 2) + square, BF),
            pltpu.VMEM((4,) + square, F32),
            pltpu.VMEM((4,) + square, F32),
            pltpu.VMEM(chain, BF),
            pltpu.VMEM(chain, BF),
            pltpu.VMEM(chain, BF),
            pltpu.VMEM(chain, BF),
            pltpu.VMEM((4, 8, 128), F32),
            pltpu.VMEM((NST, 2, 2, 2, LM // 2, HD), BF),
            pltpu.VMEM((NST, 2, 2, LM // 2, HD), BF),
            pltpu.VMEM((2, 2, 2, LM // 2, HD), F32),
            pltpu.VMEM((NST, 8, 16, 256), BF),
            pltpu.VMEM((3, NST, RUNS, RUN, 256), BF),
            pltpu.VMEM((9, 8, 128), F32),
            pltpu.VMEM((7, 8, 128), F32),
            dma((3,)), dma((7,)), dma((7,)), dma, dma,
            dma((NST, 4, 7)), dma((NST, 4, 7)), dma((NST, 4)),
            dma((3,)), dma((3,)), dma((NST,)), dma((NST,)),
            dma((NST, 2)), dma((NST, 2)), dma((NST,)), dma((NST,)),
            dma((NST,)), dma((NST,)), dma((NST, 7)), dma((NST, 7)),
            dma((NST, 3, 7)), dma((NST, 3, 7)), dma((NST, 3)), dma((NST,)),
            dma((7,)), dma((7,)), dma((3,)), dma((3,)),
        ],
        compiler_params=pltpu.CompilerParams(
            collective_id=0, has_side_effects=True, vmem_limit_bytes=56 * 2**20
        ),
        cost_estimate=pl.CostEstimate(flops=2 * 10**9, bytes_accessed=7 * 2**20, transcendentals=0),
    )(queries, key_vectors, value_vectors, cotangent, conv_weight)
    block = pl.BlockSpec((1, ROWS, full.shape[2]), lambda i: (0, i, 0))

    def whole(shape):
        return pl.BlockSpec(shape, lambda i: (0, 0))

    return pl.pallas_call(
        add_marks,
        grid=(full.shape[1] // ROWS,),
        out_shape=(full, full, full, jax.ShapeDtypeStruct(conv_weight.shape, F32)),
        in_specs=[block] * 3 + [whole(marks_grad.shape), whole(dw.shape)],
        out_specs=(block, block, block, whole(conv_weight.shape)),
        compiler_params=pltpu.CompilerParams(vmem_limit_bytes=60 * 2**20),
    )(dq, dk, dv, marks_grad, dw)


def solution(mesh):
    return jax.shard_map(
        shards,
        mesh=mesh,
        in_specs=(
            P("dp", "seq", None),
            P("dp", "seq", None),
            P("dp", "seq", None),
            P("dp", "seq", None),
            P("seq", None),
        ),
        out_specs=(
            P("dp", "seq", None),
            P("dp", "seq", None),
            P("dp", "seq", None),
            P("seq", None),
        ),
        check_vma=False,
    )
```

```python
import jax
import jax.numpy as jnp
from jax import lax
from jax.experimental import pallas as pl
from jax.experimental.pallas import tpu as pltpu
from jax.sharding import PartitionSpec as P

HD = 128
LM = 128
ITERS = 6
KW = 9
SEG = 16
SCALE = HD ** (-0.5)
MESH = pl.DeviceIdType.MESH
BF = jnp.bfloat16
F32 = jnp.float32

DP_STEPS = (1, 4, 8)
ROWS = 64
NST = 2
RUNS = 4
RUN = 256
EXT = RUN + 32
ORDER = (1, 0, 3, 2)


def dot(a, b, ca=1, cb=0):
    return lax.dot_general(a, b, (((ca,), (cb,)), ((), ())), preferred_element_type=F32)


def split(x):
    high = x.astype(BF)
    return high, (x - high.astype(F32)).astype(BF)


def mm3(a, b):
    left = jnp.concatenate([a[0], a[1], a[0]], axis=1)
    right = jnp.concatenate([b[0], b[0], b[1]], axis=0)
    return dot(left, right)


def rounded(x):
    return x.astype(BF).astype(F32)


def kernel(
    q_in, k_in, v_in, g_in, w_in,
    dq_out, dk_out, dv_out, lg_in, dw_out,
    qk_full, lm_local, lm_all, marks, w_all, taps_mat,
    land, halo, pack, pack_in, rf, rt, lf, stats, part, part_bf, part_in,
    m_save, inv_save, xt_save, p_save, p2_save, j_save, al_save,
    dkq, dkq_in, mid_grad, lg_out, out_buf, dw_buf, dw_dp,
    s_loc, s_lm, r_lm, s_lmf, r_lmf, s_in, r_in, s_own, s_w, r_w, s_ms, r_ms,
    s_part, r_part, s_halo, r_halo, s_dkq, r_dkq, s_tg, r_tg,
    s_out, r_out, s_outl, s_lgl, s_dw, r_dw, s_dp, r_dp,
):
    dp = lax.axis_index("dp")
    seq = lax.axis_index("seq")
    x = seq // 4
    z = seq % 4
    za = z // 2
    zb = z % 2
    other = 1 - za
    group = x * 2 + zb
    ins = (q_in, k_in, v_in, g_in)
    outs = (dq_out, dk_out, dv_out)
    pending = []

    def member(i):
        p = (group + i) % 8
        return p, (p // 2) * 4 + za * 2 + p % 2

    partner = x * 4 + other * 2 + zb
    cross = x * 4 + other * 2 + (1 - zb)

    def dp_peer(step):
        return dp + step - 2 * step * ((dp // step) % 2)

    def remote(src, dst, ss, rs, to, at=None):
        copy = pltpu.make_async_remote_copy(
            src_ref=src, dst_ref=dst, send_sem=ss, recv_sem=rs,
            device_id=(dp if at is None else at, to), device_id_type=MESH,
        )
        copy.start()
        pending.append(copy)
        return copy

    local = []
    for n, ref in enumerate((q_in, k_in)):
        copy = pltpu.make_async_copy(ref.at[0], qk_full.at[n], s_loc.at[n])
        copy.start()
        local.append(copy)
    w_all[...] = jnp.zeros_like(w_all)
    w_all[z, 0:2, 0:KW] = w_in[...]
    barrier = pltpu.get_barrier_semaphore()
    for i in range(1, 8):
        pl.semaphore_signal(barrier, inc=1, device_id=(dp, member(i)[1]), device_id_type=MESH)
    flip = x * 4 + za * 2 + 1 - zb
    along_z = [(dp, to) for to in (flip, partner, cross)]
    along_z += [(dp_peer(2), to) for to in (seq, flip, partner, cross)]
    for to in along_z[1:]:
        pl.semaphore_signal(barrier, inc=1, device_id=to, device_id_type=MESH)
    for step in DP_STEPS:
        pl.semaphore_signal(barrier, inc=1, device_id=(dp_peer(step), seq), device_id_type=MESH)
    pl.semaphore_wait(barrier, 16)
    in_copies = {}

    def issue(st, a):
        if st >= NST:
            return
        got = []
        spot = land.at[a, st, x, pl.ds(pl.multiple_of(zb * 128, 128), 128)]
        for i in range(1, 8):
            p, to = member(i)
            cut = pl.ds(pl.multiple_of(p * 512 + st * 256, 256), 256)
            got.append(remote(
                ins[a].at[0, :, cut], spot, s_in.at[st, a, i - 1], r_in.at[st, a, i - 1], to))
        cut = pl.ds(pl.multiple_of(group * 512 + st * 256, 256), 256)
        own = pltpu.make_async_copy(ins[a].at[0, :, cut], spot, s_own.at[st, a])
        own.start()
        in_copies[st, a] = (got, own)

    issue(0, 1)
    for copy in local:
        copy.wait()
    rows = lax.broadcasted_iota(jnp.int32, (8, 128), 0)
    cols = lax.broadcasted_iota(jnp.int32, (8, 128), 1)
    averager = jnp.where(cols // SEG == rows, 1.0 / SEG, 0.0).astype(BF)
    for c in range(8):
        cut = slice(512 * c, 512 * c + 512)
        lm_local[:, cut] = jnp.concatenate(
            [dot(averager, qk_full[0, :, cut]), dot(averager, qk_full[1, :, cut])], axis=0
        ).astype(BF)

    my_cols = pl.ds(pl.multiple_of(group * 512, 512), 512)
    lm_copies = []
    for i in range(1, 8):
        p, to = member(i)
        lm_copies.append(remote(
            lm_local.at[:, pl.ds(pl.multiple_of(p * 512, 512), 512)], lm_all.at[za, group],
            s_lm.at[i - 1], r_lm.at[i - 1], to))
    lm_own = pltpu.make_async_copy(lm_local.at[:, my_cols], lm_all.at[za, group], s_loc.at[2])
    lm_own.start()
    w_copies = [
        remote(w_all.at[z], w_all.at[z], s_w.at[n], r_w.at[n], to)
        for n, to in enumerate((x * 4 + za * 2 + 1 - zb, partner, cross))
    ]
    issue(0, 0)

    def arrive(st, a):
        got, own = in_copies[st, a]
        for copy in got:
            copy.wait_recv()
        own.wait()

    for copy in lm_copies:
        copy.wait_recv()
    lm_own.wait()
    lmf = remote(lm_all.at[za], lm_all.at[za], s_lmf, r_lmf, partner)
    issue(0, 3)
    issue(0, 2)
    for copy in w_copies:
        copy.wait_recv()

    t_at = lax.broadcasted_iota(jnp.int32, (RUN, EXT), 0)
    u_at = lax.broadcasted_iota(jnp.int32, (RUN, EXT), 1)
    for h in range(4):
        taps = w_all[2 * zb + h // 2, h % 2 : h % 2 + 1, :]
        band = jnp.zeros((RUN, EXT), F32)
        for j in range(KW):
            band = jnp.where(t_at + 20 - u_at == j, taps[:, j : j + 1], band)
        high, low = split(band)
        taps_mat[h, 0] = high
        taps_mat[h, 1] = low

    lmf.wait_recv()
    lm_values = lm_all[...].astype(F32)
    for h in range(4):
        piece = lm_values[:, :, :, 128 * h : 128 * h + 128]
        marks[0, h] = piece[:, :, 0:8].reshape(LM, HD).astype(BF)
        marks[1, h] = piece[:, :, 8:16].reshape(LM, HD).astype(BF)

    r_at = lax.broadcasted_iota(jnp.int32, (LM, LM), 0)
    c_at = lax.broadcasted_iota(jnp.int32, (LM, LM), 1)
    eye = jnp.where(r_at == c_at, 1.0, 0.0).astype(F32)

    def invert(st):
        state = []
        for h in (2 * st, 2 * st + 1):
            logits = dot(marks[0, h], marks[1, h], 1, 1) * SCALE
            e = jnp.exp(logits - jnp.max(logits, axis=1, keepdims=True))
            middle = e / jnp.sum(e, axis=1, keepdims=True)
            top = jnp.max(jnp.sum(middle, axis=0, keepdims=True), axis=1, keepdims=True)
            side = jnp.max(jnp.sum(middle, axis=1, keepdims=True), axis=0, keepdims=True)
            al = 1.0 / (top * side)
            m_save[h] = middle
            al_save[h] = jnp.broadcast_to(al, (8, 128))
            x0 = al * middle.T
            state.append([x0, mm3(split(middle), split(x0))])
        for it in range(ITERS):
            for j in range(2):
                inv, prod = state[j]
                h = 2 * st + j
                ps = split(prod)
                prod2 = mm3(ps, ps)
                p2s = split(prod2)
                j_mat = 13.0 * eye - 15.0 * prod + mm3(p2s, split(7.0 * eye - prod))
                js = split(j_mat)
                xts = split(inv.T)
                for n in range(2):
                    xt_save[h, it, n] = xts[n]
                    p_save[h, it, n] = ps[n]
                    p2_save[h, it, n] = p2s[n]
                    j_save[h, it, n] = js[n]
                new = 0.25 * mm3(split(inv), js)
                if it < ITERS - 1:
                    prod = 0.25 * (13.0 * prod - 15.0 * prod2 + mm3(p2s, split(7.0 * prod - prod2)))
                state[j] = [new, prod]
        for j in range(2):
            inv_save[2 * st + j] = state[j][0]

    dw_state = {}

    def dw_start():
        place = (dp // 2) % 2 * 4 + z
        dw_buf[place] = dw_buf[8]
        dw_state["z"] = [
            remote(dw_buf.at[8], dw_buf.at[place], s_dw.at[n], r_dw.at[n], to, at=at)
            for n, (at, to) in enumerate(along_z)
        ]

    def dw_step(b):
        if b == 0:
            for copy in dw_state["z"]:
                copy.wait_recv()
            first = dw_buf[z // 2] + dw_buf[z // 2 + 2]
            both = first + (dw_buf[z // 2 + 4] + dw_buf[z // 2 + 6])
            dw_dp[0] = jnp.where(z % 2 == 0, both, jnp.concatenate([both[2:8], both[0:2]], axis=0))
        else:
            dw_state["dp"].wait_recv()
            dw_dp[2 * b] = dw_dp[2 * b - 2] + dw_dp[2 * b - 1]
        if b < 3:
            dw_state["dp"] = remote(
                dw_dp.at[2 * b], dw_dp.at[2 * b + 1], s_dp.at[b], r_dp.at[b], seq,
                at=dp_peer(DP_STEPS[b]))
        else:
            dw_out[...] = dw_dp[6]

    at64, at16 = (lax.broadcasted_iota(jnp.int32, (16, n), 1) for n in (64, 16))
    to64, to16 = (lax.broadcasted_iota(jnp.int32, (16, n), 0) for n in (64, 16))

    def ones_where(cond):
        return jnp.where(cond, 1.0, 0.0).astype(BF)

    pick_first = ones_where(at64 == (to64 // 4) * 16 + to64 % 4)
    pick_final = ones_where(at64 == (to64 // 4) * 16 + 12 + to64 % 4)
    spread = (
        [ones_where((at16 // 4 == r - 1 + za) & (to16 == 12 + at16 % 4)) for r in range(RUNS)],
        [ones_where((at16 // 4 == r + za) & (to16 == at16 % 4)) for r in range(RUNS)],
    )
    dw_buf[8] = jnp.zeros((8, 128), F32)
    lane = lax.broadcasted_iota(jnp.int32, (1, 128), 1)

    out_copies = {(st, a): [] for st in range(NST) for a in range(3)}
    own_out = {}
    lg_copies = {}

    def finish(st):
        for copy in lg_copies[st]:
            copy.wait_recv()
        for a in (2, 1, 0):
            for copy in out_copies[st, a]:
                copy.wait_recv()
            own_out[st, a].wait()
        own_out[st, 3].wait()

    def head(st, a, j):
        return land[a, st, :, :, 128 * j : 128 * j + 128].reshape(RUNS * RUN, HD)

    def send_halo(st):
        first = land[3, st, :, 0:16, :].reshape(RUNS * 16, 256)
        final = land[3, st, :, RUN - 16 : RUN, :].reshape(RUNS * 16, 256)
        pack[st, 0] = dot(pick_final, final).astype(BF)
        pack[st, 1] = dot(pick_first, first).astype(BF)
        return remote(pack.at[st], pack_in.at[st], s_halo.at[st], r_halo.at[st], partner)

    def extended(st, r, j):
        cut = slice(128 * j, 128 * j + 128)
        return jnp.concatenate(
            [halo[st, 0, r, :, cut], land[3, st, r, :, cut], halo[st, 1, r, :, cut]], axis=0)

    sent = {}

    def prepare(st):
        arrive(st, 1)
        for j in range(2):
            logits = dot(head(st, 1, j), marks[0, 2 * st + j], 1, 1) * SCALE
            m = jnp.max(logits, axis=0, keepdims=True)
            e = jnp.exp(logits - m)
            rf[st, j] = e
            stats[st, za, 2 * j : 2 * j + 1, :] = m
            stats[st, za, 2 * j + 1 : 2 * j + 2, :] = jnp.sum(e, axis=0, keepdims=True)
        ms = remote(stats.at[st, za], stats.at[st, za], s_ms.at[st], r_ms.at[st], partner)
        if st == 0:
            issue(1, 1)
            issue(1, 0)
        arrive(st, 0)
        for j in range(2):
            logits = dot(marks[1, 2 * st + j], head(st, 0, j), 1, 1) * SCALE
            e = jnp.exp(logits - jnp.max(logits, axis=0, keepdims=True))
            lf[st, j] = e * (1.0 / jnp.sum(e, axis=0, keepdims=True))
        invert(st)
        arrive(st, 3)
        for j in range(2):
            part[st, 0, j] = dot(lf[st, j].astype(BF), head(st, 3, j))
            part_bf[st, 0, j] = part[st, 0, j].astype(BF)
        sent[st, "dm"] = remote(
            part_bf.at[st, 0], part_in.at[st, 0], s_part.at[st, 0], r_part.at[st, 0], partner)
        sent[st, "halo"] = send_halo(st)
        sent[st, "ms"] = ms

    def sum_up(st):
        sent[st, "ms"].wait_recv()
        for j in range(2):
            m1 = stats[st, za, 2 * j : 2 * j + 1, :]
            s1 = stats[st, za, 2 * j + 1 : 2 * j + 2, :]
            m2 = stats[st, other, 2 * j : 2 * j + 1, :]
            s2 = stats[st, other, 2 * j + 1 : 2 * j + 2, :]
            m = jnp.maximum(m1, m2)
            e1 = jnp.exp(m1 - m)
            factor = e1 / (s1 * e1 + s2 * jnp.exp(m2 - m))
            value = rf[st, j] * factor
            rf[st, j] = value
            rt[st, j] = value.astype(BF)
        arrive(st, 2)
        for j in range(2):
            part[st, 1, j] = dot(rt[st, j], head(st, 2, j), 0, 0)
            part_bf[st, 1, j] = part[st, 1, j].astype(BF)
        sent[st, "sum"] = remote(
            part_bf.at[st, 1], part_in.at[st, 1], s_part.at[st, 1], r_part.at[st, 1], partner)

    def convolve(st):
        sent[st, "halo"].wait_recv()
        for side in range(2):
            packed = pack_in[st, side]
            for r in range(RUNS):
                halo[st, side, r] = dot(spread[side][r], packed).astype(BF)
        for j in range(2):
            for r in range(RUNS):
                g_ext = extended(st, r, j)
                conv = dot(taps_mat[2 * st + j, 0], g_ext) + dot(taps_mat[2 * st + j, 1], g_ext)
                out_buf[2, st, r, :, 128 * j : 128 * j + 128] = conv.astype(BF)

    def taps_grad(st):
        for j in range(2):
            corr = jnp.zeros((RUN, EXT), F32)
            for r in range(RUNS):
                cut = slice(128 * j, 128 * j + 128)
                corr += dot(land[2, st, r, :, cut], extended(st, r, j), 1, 1)
            line = jnp.zeros((1, 128), F32)
            for t in range(KW):
                band = jnp.where(t_at + 20 - u_at == t, corr, 0.0)
                total = jnp.sum(jnp.sum(band, axis=0, keepdims=True), axis=1, keepdims=True)
                line = jnp.where(lane == t, total, line)
            dw_buf[8, 2 * st + j : 2 * st + j + 1, :] = line

    def totals(st, j):
        dms = (part[st, 0, j] + part_in[st, 0, j].astype(F32)).astype(BF)
        return dms, part[st, 1, j] + part_in[st, 1, j].astype(F32)

    def send_out(st, a):
        spot = outs[a].at[0, :, pl.ds(pl.multiple_of(group * 512 + st * 256, 256), 256)]
        for i in range(1, 8):
            p, to = member(i)
            out_copies[st, a].append(remote(
                out_buf.at[a, st, p // 2, pl.ds(pl.multiple_of((p % 2) * 128, 128), 128)], spot,
                s_out.at[st, a, i - 1], r_out.at[st, a, i - 1], to))
        copy = pltpu.make_async_copy(
            out_buf.at[a, st, x, pl.ds(pl.multiple_of(zb * 128, 128), 128)], spot,
            s_outl.at[st, a])
        copy.start()
        own_out[st, a] = copy

    def grads(st):
        sent[st, "dm"].wait_recv()
        sent[st, "sum"].wait_recv()
        mixeds, dsums, deltas = [], [], []
        for j in range(2):
            dms, summary = totals(st, j)
            inv = inv_save[2 * st + j]
            inv_t = split(inv.T)
            mixed = jnp.dot(
                inv, summary, precision=lax.Precision.HIGHEST, preferred_element_type=F32)
            dsum = dot(jnp.concatenate([inv_t[0], inv_t[1]], axis=1),
                       jnp.concatenate([dms, dms], axis=0))
            mixeds.append(mixed.astype(BF))
            dsums.append(dsum.astype(BF))
            deltas.append(jnp.sum((dsum * summary).T, axis=0, keepdims=True))
        for j in range(2):
            cut = slice(128 * j, 128 * j + 128)
            d_v = rounded(dot(rt[st, j], dsums[j])).reshape(RUNS, RUN, HD)
            out_buf[2, st, :, :, cut] = (out_buf[2, st, :, :, cut].astype(F32) + d_v).astype(BF)
        send_out(st, 2)
        for j in range(2):
            cut = slice(128 * j, 128 * j + 128)
            d_right = rounded(dot(head(st, 2, j), dsums[j], 1, 1))
            d_right = (rf[st, j] * (d_right - deltas[j]) * SCALE).astype(BF)
            d_k = dot(d_right, marks[0, 2 * st + j]).astype(BF)
            out_buf[1, st, :, :, cut] = d_k.reshape(RUNS, RUN, HD)
            dkq[st, 0, :, j] = dot(d_right, head(st, 1, j), 0, 0).astype(BF).reshape(
                2, LM // 2, HD)
        for j in range(2):
            cut = slice(128 * j, 128 * j + 128)
            left = lf[st, j]
            d_left = rounded(dot(mixeds[j], head(st, 3, j), 1, 1))
            prod = left * d_left
            d_left = ((prod - left * jnp.sum(prod, axis=0, keepdims=True)) * SCALE).astype(BF)
            d_q = dot(d_left, marks[1, 2 * st + j], 0, 0).astype(BF)
            out_buf[0, st, :, :, cut] = d_q.reshape(RUNS, RUN, HD)
            dkq[st, 1, :, j] = dot(d_left, head(st, 0, j)).astype(BF).reshape(2, LM // 2, HD)
        sent[st, "dkq"] = remote(
            dkq.at[st, :, other], dkq_in.at[st], s_dkq.at[st], r_dkq.at[st], partner)

    def reverse(st):
        chain = []
        for j in range(2):
            dms, summary = totals(st, j)
            s_t = split(summary.T)
            grad = dot(
                jnp.concatenate([dms, dms], axis=1), jnp.concatenate([s_t[0], s_t[1]], axis=0))
            chain.append([grad, jnp.zeros((LM, LM), F32), split(m_save[2 * st + j].T)])
        for it in reversed(range(ITERS)):
            for j in range(2):
                h = 2 * st + j
                grad, d_mid, m_t = chain[j]
                xt = (xt_save[h, it, 0], xt_save[h, it, 1])
                ps = (p_save[h, it, 0], p_save[h, it, 1])
                p2s = (p2_save[h, it, 0], p2_save[h, it, 1])
                js = (j_save[h, it, 0], j_save[h, it, 1])
                ws = split(grad)
                g_mat = 0.25 * mm3(xt, ws)
                gs = split(g_mat)
                u_mat = 7.0 * g_mat - mm3(gs, ps)
                us = split(u_mat)
                d_p = mm3(us, ps) + mm3(ps, us) - mm3(p2s, gs) - 15.0 * g_mat
                dps = split(d_p)
                d_mid = d_mid + mm3(dps, xt)
                grad = 0.25 * mm3(ws, js) + mm3(m_t, dps)
                chain[j] = [grad, d_mid, m_t]
        for j in range(2):
            h = 2 * st + j
            grad, d_mid, m_t = chain[j]
            middle = m_save[h]
            d_mid = d_mid + al_save[h, 0:1, :] * grad.T
            d_log = middle * (d_mid - jnp.sum(middle * d_mid, axis=1, keepdims=True)) * SCALE
            d_log = d_log.astype(BF)
            mid_grad[st, 0, j] = dot(d_log, marks[1, h]).reshape(2, LM // 2, HD)
            mid_grad[st, 1, j] = dot(d_log, marks[0, h], 0, 0).reshape(2, LM // 2, HD)

    def send_marks(st):
        sent[st, "dkq"].wait_recv()
        for j in range(2):
            cut = slice(128 * j, 128 * j + 128)
            both = []
            for n in range(2):
                rest = rounded(dkq[st, n, za, j].astype(F32) + dkq_in[st, n, j].astype(F32))
                rest = rounded(rest + rounded(mid_grad[st, n, j, za])) * (1.0 / SEG)
                both.append(rest.reshape(8, 8, HD))
            lg_out[st, :, :, cut] = jnp.concatenate(both, axis=1).astype(BF)
        lg_copies[st] = []
        spot = pl.ds(pl.multiple_of(group * 512 + st * 256, 256), 256)
        for i in range(1, 8):
            p, to = member(i)
            lg_copies[st].append(remote(
                lg_out.at[st, p], lg_in.at[:, spot], s_tg.at[st, i - 1], r_tg.at[st, i - 1], to))
        own = pltpu.make_async_copy(lg_out.at[st, group], lg_in.at[:, spot], s_lgl.at[st])
        own.start()
        own_out[st, 3] = own

    prepare(0)
    sum_up(0)
    issue(1, 3)
    issue(1, 2)
    prepare(1)
    convolve(0)
    grads(0)
    sum_up(1)
    convolve(1)
    taps_grad(0)
    taps_grad(1)
    dw_start()
    send_out(0, 1)
    send_out(0, 0)
    reverse(0)
    grads(1)
    send_out(1, 1)
    send_out(1, 0)
    send_marks(0)
    reverse(1)
    send_marks(1)
    dw_step(0)
    dw_step(1)
    dw_step(2)
    for st in range(NST):
        finish(st)
    dw_step(3)
    for copy in pending:
        copy.wait_send()


def add_marks(dq, dk, dv, marks_grad, dw, dq_out, dk_out, dv_out, dw_out):
    at = (pl.program_id(0) * ROWS + lax.broadcasted_iota(jnp.int32, (ROWS, 16), 0)) // SEG
    col = lax.broadcasted_iota(jnp.int32, (ROWS, 16), 1)
    for n, (part, out) in enumerate(((dq, dq_out), (dk, dk_out))):
        pick = jnp.where(col == at + 8 * n, 1.0, 0.0).astype(BF)
        out[0] = (part[0].astype(F32) + dot(pick, marks_grad[...])).astype(BF)
    dv_out[...] = dv[...]
    dw_out[...] = dw[0:2, 0:KW]


def shards(queries, key_vectors, value_vectors, cotangent, conv_weight):
    any_spec = pl.BlockSpec(memory_space=pl.ANY)
    vmem_spec = pl.BlockSpec(memory_space=pltpu.VMEM)
    full = jax.ShapeDtypeStruct(queries.shape, BF)
    dma = pltpu.SemaphoreType.DMA
    square = (LM, HD)
    chain = (4, ITERS, 2) + square
    dq, dk, dv, marks_grad, dw = pl.pallas_call(
        kernel,
        out_shape=(
            full, full, full, jax.ShapeDtypeStruct((16, full.shape[2]), BF),
            jax.ShapeDtypeStruct((8, 128), F32)),
        in_specs=[any_spec] * 4 + [vmem_spec],
        out_specs=(any_spec,) * 4 + (vmem_spec,),
        scratch_shapes=[
            pltpu.VMEM((2, 128, 4096), BF),
            pltpu.VMEM((16, 4096), BF),
            pltpu.VMEM((2, 8, 16, 512), BF),
            pltpu.VMEM((2, 4) + square, BF),
            pltpu.VMEM((4, 8, 128), F32),
            pltpu.VMEM((4, 2, RUN, EXT), BF),
            pltpu.VMEM((4, NST, RUNS, RUN, 256), BF),
            pltpu.VMEM((NST, 2, RUNS, 16, 256), BF),
            pltpu.VMEM((NST, 2, 16, 256), BF),
            pltpu.VMEM((NST, 2, 16, 256), BF),
            pltpu.VMEM((NST, 2, RUNS * RUN, LM), F32),
            pltpu.VMEM((NST, 2, RUNS * RUN, LM), BF),
            pltpu.VMEM((NST, 2, LM, RUNS * RUN), F32),
            pltpu.VMEM((NST, 2, 8, 128), F32),
            pltpu.VMEM((NST, 2, 2) + square, F32),
            pltpu.VMEM((NST, 2, 2) + square, BF),
            pltpu.VMEM((NST, 2, 2) + square, BF),
            pltpu.VMEM((4,) + square, F32),
            pltpu.VMEM((4,) + square, F32),
            pltpu.VMEM(chain, BF),
            pltpu.VMEM(chain, BF),
            pltpu.VMEM(chain, BF),
            pltpu.VMEM(chain, BF),
            pltpu.VMEM((4, 8, 128), F32),
            pltpu.VMEM((NST, 2, 2, 2, LM // 2, HD), BF),
            pltpu.VMEM((NST, 2, 2, LM // 2, HD), BF),
            pltpu.VMEM((NST, 2, 2, 2, LM // 2, HD), F32),
            pltpu.VMEM((NST, 8, 16, 256), BF),
            pltpu.VMEM((3, NST, RUNS, RUN, 256), BF),
            pltpu.VMEM((9, 8, 128), F32),
            pltpu.VMEM((7, 8, 128), F32),
            dma((3,)), dma((7,)), dma((7,)), dma, dma,
            dma((NST, 4, 7)), dma((NST, 4, 7)), dma((NST, 4)),
            dma((3,)), dma((3,)), dma((NST,)), dma((NST,)),
            dma((NST, 2)), dma((NST, 2)), dma((NST,)), dma((NST,)),
            dma((NST,)), dma((NST,)), dma((NST, 7)), dma((NST, 7)),
            dma((NST, 3, 7)), dma((NST, 3, 7)), dma((NST, 3)), dma((NST,)),
            dma((7,)), dma((7,)), dma((3,)), dma((3,)),
        ],
        compiler_params=pltpu.CompilerParams(
            collective_id=0, has_side_effects=True, vmem_limit_bytes=50 * 2**20
        ),
        cost_estimate=pl.CostEstimate(flops=2 * 10**9, bytes_accessed=7 * 2**20, transcendentals=0),
    )(queries, key_vectors, value_vectors, cotangent, conv_weight)
    block = pl.BlockSpec((1, ROWS, full.shape[2]), lambda i: (0, i, 0))

    def whole(shape):
        return pl.BlockSpec(shape, lambda i: (0, 0))

    return pl.pallas_call(
        add_marks,
        grid=(full.shape[1] // ROWS,),
        out_shape=(full, full, full, jax.ShapeDtypeStruct(conv_weight.shape, F32)),
        in_specs=[block] * 3 + [whole(marks_grad.shape), whole(dw.shape)],
        out_specs=(block, block, block, whole(conv_weight.shape)),
        compiler_params=pltpu.CompilerParams(vmem_limit_bytes=30 * 2**20),
    )(dq, dk, dv, marks_grad, dw)


def solution(mesh):
    return jax.shard_map(
        shards,
        mesh=mesh,
        in_specs=(
            P("dp", "seq", None),
            P("dp", "seq", None),
            P("dp", "seq", None),
            P("dp", "seq", None),
            P("seq", None),
        ),
        out_specs=(
            P("dp", "seq", None),
            P("dp", "seq", None),
            P("dp", "seq", None),
            P("seq", None),
        ),
        check_vma=False,
    )
```

```python
import jax
import jax.numpy as jnp
from jax import lax
from jax.experimental import pallas as pl
from jax.experimental.pallas import tpu as pltpu
from jax.sharding import PartitionSpec as P

HD = 128
LM = 128
ITERS = 6
KW = 9
SEG = 16
SCALE = HD ** (-0.5)
MESH = pl.DeviceIdType.MESH
BF = jnp.bfloat16
F32 = jnp.float32

DP_STEPS = (1, 4, 8)
ROWS = 32
NST = 2
RUNS = 4
RUN = 256
EXT = RUN + 32
ORDER = (1, 0, 3, 2)


def dot(a, b, ca=1, cb=0):
    return lax.dot_general(a, b, (((ca,), (cb,)), ((), ())), preferred_element_type=F32)


def split(x):
    high = x.astype(BF)
    return high, (x - high.astype(F32)).astype(BF)


def mm3(a, b):
    left = jnp.concatenate([a[0], a[1], a[0]], axis=1)
    right = jnp.concatenate([b[0], b[0], b[1]], axis=0)
    return dot(left, right)


def rounded(x):
    return x.astype(BF).astype(F32)


def kernel(
    q_in, k_in, v_in, g_in, w_in,
    dq_out, dk_out, dv_out, lg_in, dw_out,
    qk_full, lm_local, lm_all, marks, w_all, taps_mat,
    land, halo, pack, pack_in, rf, rt, lf, stats, part, part_bf, part_in,
    m_save, inv_save, xt_save, p_save, p2_save, j_save, al_save,
    dkq, dkq_in, mid_grad, lg_out, out_buf, dw_buf, dw_dp,
    s_loc, s_lm, r_lm, s_lmf, r_lmf, s_in, r_in, s_own, s_w, r_w, s_ms, r_ms,
    s_part, r_part, s_halo, r_halo, s_dkq, r_dkq, s_tg, r_tg,
    s_out, r_out, s_outl, s_lgl, s_dw, r_dw, s_dp, r_dp,
):
    dp = lax.axis_index("dp")
    seq = lax.axis_index("seq")
    x = seq // 4
    z = seq % 4
    za = z // 2
    zb = z % 2
    other = 1 - za
    group = x * 2 + zb
    ins = (q_in, k_in, v_in, g_in)
    outs = (dq_out, dk_out, dv_out)
    pending = []

    def member(i):
        p = (group + i) % 8
        return p, (p // 2) * 4 + za * 2 + p % 2

    partner = x * 4 + other * 2 + zb
    cross = x * 4 + other * 2 + (1 - zb)

    def dp_peer(step):
        return dp + step - 2 * step * ((dp // step) % 2)

    def remote(src, dst, ss, rs, to, at=None):
        copy = pltpu.make_async_remote_copy(
            src_ref=src, dst_ref=dst, send_sem=ss, recv_sem=rs,
            device_id=(dp if at is None else at, to), device_id_type=MESH,
        )
        copy.start()
        pending.append(copy)
        return copy

    local = []
    for n, ref in enumerate((q_in, k_in)):
        copy = pltpu.make_async_copy(ref.at[0], qk_full.at[n], s_loc.at[n])
        copy.start()
        local.append(copy)
    w_all[...] = jnp.zeros_like(w_all)
    w_all[z, 0:2, 0:KW] = w_in[...]
    barrier = pltpu.get_barrier_semaphore()
    for i in range(1, 8):
        pl.semaphore_signal(barrier, inc=1, device_id=(dp, member(i)[1]), device_id_type=MESH)
    flip = x * 4 + za * 2 + 1 - zb
    along_z = [(dp, to) for to in (flip, partner, cross)]
    along_z += [(dp_peer(2), to) for to in (seq, flip, partner, cross)]
    for to in along_z[1:]:
        pl.semaphore_signal(barrier, inc=1, device_id=to, device_id_type=MESH)
    for step in DP_STEPS:
        pl.semaphore_signal(barrier, inc=1, device_id=(dp_peer(step), seq), device_id_type=MESH)
    pl.semaphore_wait(barrier, 16)
    in_copies = {}

    def issue(st, a):
        if st >= NST:
            return
        got = []
        spot = land.at[a, st, x, pl.ds(pl.multiple_of(zb * 128, 128), 128)]
        for i in range(1, 8):
            p, to = member(i)
            cut = pl.ds(pl.multiple_of(p * 512 + st * 256, 256), 256)
            got.append(remote(
                ins[a].at[0, :, cut], spot, s_in.at[st, a, i - 1], r_in.at[st, a, i - 1], to))
        cut = pl.ds(pl.multiple_of(group * 512 + st * 256, 256), 256)
        own = pltpu.make_async_copy(ins[a].at[0, :, cut], spot, s_own.at[st, a])
        own.start()
        in_copies[st, a] = (got, own)

    issue(0, 1)
    for copy in local:
        copy.wait()
    rows = lax.broadcasted_iota(jnp.int32, (8, 128), 0)
    cols = lax.broadcasted_iota(jnp.int32, (8, 128), 1)
    averager = jnp.where(cols // SEG == rows, 1.0 / SEG, 0.0).astype(BF)
    for c in range(8):
        cut = slice(512 * c, 512 * c + 512)
        lm_local[:, cut] = jnp.concatenate(
            [dot(averager, qk_full[0, :, cut]), dot(averager, qk_full[1, :, cut])], axis=0
        ).astype(BF)

    my_cols = pl.ds(pl.multiple_of(group * 512, 512), 512)
    lm_copies = []
    for i in range(1, 8):
        p, to = member(i)
        lm_copies.append(remote(
            lm_local.at[:, pl.ds(pl.multiple_of(p * 512, 512), 512)], lm_all.at[za, group],
            s_lm.at[i - 1], r_lm.at[i - 1], to))
    lm_own = pltpu.make_async_copy(lm_local.at[:, my_cols], lm_all.at[za, group], s_loc.at[2])
    lm_own.start()
    w_copies = [
        remote(w_all.at[z], w_all.at[z], s_w.at[n], r_w.at[n], to)
        for n, to in enumerate((x * 4 + za * 2 + 1 - zb, partner, cross))
    ]
    issue(0, 0)

    def arrive(st, a):
        got, own = in_copies[st, a]
        for copy in got:
            copy.wait_recv()
        own.wait()

    for copy in lm_copies:
        copy.wait_recv()
    lm_own.wait()
    lmf = remote(lm_all.at[za], lm_all.at[za], s_lmf, r_lmf, partner)
    issue(0, 3)
    issue(0, 2)
    for copy in w_copies:
        copy.wait_recv()

    t_at = lax.broadcasted_iota(jnp.int32, (RUN, EXT), 0)
    u_at = lax.broadcasted_iota(jnp.int32, (RUN, EXT), 1)
    for h in range(4):
        taps = w_all[2 * zb + h // 2, h % 2 : h % 2 + 1, :]
        band = jnp.zeros((RUN, EXT), F32)
        for j in range(KW):
            band = jnp.where(t_at + 20 - u_at == j, taps[:, j : j + 1], band)
        high, low = split(band)
        taps_mat[h, 0] = high
        taps_mat[h, 1] = low

    lmf.wait_recv()
    lm_values = lm_all[...].astype(F32)
    for h in range(4):
        piece = lm_values[:, :, :, 128 * h : 128 * h + 128]
        marks[0, h] = piece[:, :, 0:8].reshape(LM, HD).astype(BF)
        marks[1, h] = piece[:, :, 8:16].reshape(LM, HD).astype(BF)

    r_at = lax.broadcasted_iota(jnp.int32, (LM, LM), 0)
    c_at = lax.broadcasted_iota(jnp.int32, (LM, LM), 1)
    eye = jnp.where(r_at == c_at, 1.0, 0.0).astype(F32)

    def invert(st):
        state = []
        for h in (2 * st, 2 * st + 1):
            logits = dot(marks[0, h], marks[1, h], 1, 1) * SCALE
            e = jnp.exp(logits - jnp.max(logits, axis=1, keepdims=True))
            middle = e / jnp.sum(e, axis=1, keepdims=True)
            top = jnp.max(jnp.sum(middle, axis=0, keepdims=True), axis=1, keepdims=True)
            side = jnp.max(jnp.sum(middle, axis=1, keepdims=True), axis=0, keepdims=True)
            al = 1.0 / (top * side)
            m_save[h] = middle
            al_save[h] = jnp.broadcast_to(al, (8, 128))
            x0 = al * middle.T
            state.append([x0, mm3(split(middle), split(x0))])
        for it in range(ITERS):
            for j in range(2):
                inv, prod = state[j]
                h = 2 * st + j
                ps = split(prod)
                prod2 = mm3(ps, ps)
                p2s = split(prod2)
                j_mat = 13.0 * eye - 15.0 * prod + mm3(p2s, split(7.0 * eye - prod))
                js = split(j_mat)
                xts = split(inv.T)
                for n in range(2):
                    xt_save[h, it, n] = xts[n]
                    p_save[h, it, n] = ps[n]
                    p2_save[h, it, n] = p2s[n]
                    j_save[h, it, n] = js[n]
                new = 0.25 * mm3(split(inv), js)
                if it < ITERS - 1:
                    prod = 0.25 * (13.0 * prod - 15.0 * prod2 + mm3(p2s, split(7.0 * prod - prod2)))
                state[j] = [new, prod]
        for j in range(2):
            inv_save[2 * st + j] = state[j][0]

    dw_state = {}

    def dw_start():
        place = (dp // 2) % 2 * 4 + z
        dw_buf[place] = dw_buf[8]
        dw_state["z"] = [
            remote(dw_buf.at[8], dw_buf.at[place], s_dw.at[n], r_dw.at[n], to, at=at)
            for n, (at, to) in enumerate(along_z)
        ]

    def dw_step(b):
        if b == 0:
            for copy in dw_state["z"]:
                copy.wait_recv()
            first = dw_buf[z // 2] + dw_buf[z // 2 + 2]
            both = first + (dw_buf[z // 2 + 4] + dw_buf[z // 2 + 6])
            dw_dp[0] = jnp.where(z % 2 == 0, both, jnp.concatenate([both[2:8], both[0:2]], axis=0))
        else:
            dw_state["dp"].wait_recv()
            dw_dp[2 * b] = dw_dp[2 * b - 2] + dw_dp[2 * b - 1]
        if b < 3:
            dw_state["dp"] = remote(
                dw_dp.at[2 * b], dw_dp.at[2 * b + 1], s_dp.at[b], r_dp.at[b], seq,
                at=dp_peer(DP_STEPS[b]))
        else:
            dw_out[...] = dw_dp[6]

    at64, at16 = (lax.broadcasted_iota(jnp.int32, (16, n), 1) for n in (64, 16))
    to64, to16 = (lax.broadcasted_iota(jnp.int32, (16, n), 0) for n in (64, 16))

    def ones_where(cond):
        return jnp.where(cond, 1.0, 0.0).astype(BF)

    pick_first = ones_where(at64 == (to64 // 4) * 16 + to64 % 4)
    pick_final = ones_where(at64 == (to64 // 4) * 16 + 12 + to64 % 4)
    spread = (
        [ones_where((at16 // 4 == r - 1 + za) & (to16 == 12 + at16 % 4)) for r in range(RUNS)],
        [ones_where((at16 // 4 == r + za) & (to16 == at16 % 4)) for r in range(RUNS)],
    )
    dw_buf[8] = jnp.zeros((8, 128), F32)
    lane = lax.broadcasted_iota(jnp.int32, (1, 128), 1)

    out_copies = {(st, a): [] for st in range(NST) for a in range(3)}
    own_out = {}
    lg_copies = {}

    def finish(st):
        for copy in lg_copies[st]:
            copy.wait_recv()
        for a in (2, 1, 0):
            for copy in out_copies[st, a]:
                copy.wait_recv()
            own_out[st, a].wait()
        own_out[st, 3].wait()

    def head(st, a, j):
        return land[a, st, :, :, 128 * j : 128 * j + 128].reshape(RUNS * RUN, HD)

    def send_halo(st):
        first = land[3, st, :, 0:16, :].reshape(RUNS * 16, 256)
        final = land[3, st, :, RUN - 16 : RUN, :].reshape(RUNS * 16, 256)
        pack[st, 0] = dot(pick_final, final).astype(BF)
        pack[st, 1] = dot(pick_first, first).astype(BF)
        return remote(pack.at[st], pack_in.at[st], s_halo.at[st], r_halo.at[st], partner)

    def extended(st, r, j):
        cut = slice(128 * j, 128 * j + 128)
        return jnp.concatenate(
            [halo[st, 0, r, :, cut], land[3, st, r, :, cut], halo[st, 1, r, :, cut]], axis=0)

    sent = {}

    def prepare(st):
        arrive(st, 1)
        for j in range(2):
            logits = dot(head(st, 1, j), marks[0, 2 * st + j], 1, 1) * SCALE
            m = jnp.max(logits, axis=0, keepdims=True)
            e = jnp.exp(logits - m)
            rf[st, j] = e
            stats[st, za, 2 * j : 2 * j + 1, :] = m
            stats[st, za, 2 * j + 1 : 2 * j + 2, :] = jnp.sum(e, axis=0, keepdims=True)
        ms = remote(stats.at[st, za], stats.at[st, za], s_ms.at[st], r_ms.at[st], partner)
        if st == 0:
            issue(1, 1)
            issue(1, 0)
        arrive(st, 0)
        for j in range(2):
            logits = dot(marks[1, 2 * st + j], head(st, 0, j), 1, 1) * SCALE
            e = jnp.exp(logits - jnp.max(logits, axis=0, keepdims=True))
            lf[st, j] = e * (1.0 / jnp.sum(e, axis=0, keepdims=True))
        invert(st)
        arrive(st, 3)
        for j in range(2):
            part[st, 0, j] = dot(lf[st, j].astype(BF), head(st, 3, j))
            part_bf[st, 0, j] = part[st, 0, j].astype(BF)
        sent[st, "dm"] = remote(
            part_bf.at[st, 0], part_in.at[st, 0], s_part.at[st, 0], r_part.at[st, 0], partner)
        sent[st, "halo"] = send_halo(st)
        sent[st, "ms"] = ms

    def sum_up(st):
        sent[st, "ms"].wait_recv()
        for j in range(2):
            m1 = stats[st, za, 2 * j : 2 * j + 1, :]
            s1 = stats[st, za, 2 * j + 1 : 2 * j + 2, :]
            m2 = stats[st, other, 2 * j : 2 * j + 1, :]
            s2 = stats[st, other, 2 * j + 1 : 2 * j + 2, :]
            m = jnp.maximum(m1, m2)
            e1 = jnp.exp(m1 - m)
            factor = e1 / (s1 * e1 + s2 * jnp.exp(m2 - m))
            value = rf[st, j] * factor
            rf[st, j] = value
            rt[st, j] = value.astype(BF)
        arrive(st, 2)
        for j in range(2):
            part[st, 1, j] = dot(rt[st, j], head(st, 2, j), 0, 0)
            part_bf[st, 1, j] = part[st, 1, j].astype(BF)
        sent[st, "sum"] = remote(
            part_bf.at[st, 1], part_in.at[st, 1], s_part.at[st, 1], r_part.at[st, 1], partner)

    def convolve(st):
        sent[st, "halo"].wait_recv()
        for side in range(2):
            packed = pack_in[st, side]
            for r in range(RUNS):
                halo[st, side, r] = dot(spread[side][r], packed).astype(BF)
        for j in range(2):
            for r in range(RUNS):
                g_ext = extended(st, r, j)
                conv = dot(taps_mat[2 * st + j, 0], g_ext) + dot(taps_mat[2 * st + j, 1], g_ext)
                out_buf[2, st, r, :, 128 * j : 128 * j + 128] = conv.astype(BF)

    def taps_grad(st):
        for j in range(2):
            corr = jnp.zeros((RUN, EXT), F32)
            for r in range(RUNS):
                cut = slice(128 * j, 128 * j + 128)
                corr += dot(land[2, st, r, :, cut], extended(st, r, j), 1, 1)
            line = jnp.zeros((1, 128), F32)
            for t in range(KW):
                band = jnp.where(t_at + 20 - u_at == t, corr, 0.0)
                total = jnp.sum(jnp.sum(band, axis=0, keepdims=True), axis=1, keepdims=True)
                line = jnp.where(lane == t, total, line)
            dw_buf[8, 2 * st + j : 2 * st + j + 1, :] = line

    def totals(st, j):
        dms = (part[st, 0, j] + part_in[st, 0, j].astype(F32)).astype(BF)
        return dms, part[st, 1, j] + part_in[st, 1, j].astype(F32)

    def send_out(st, a):
        spot = outs[a].at[0, :, pl.ds(pl.multiple_of(group * 512 + st * 256, 256), 256)]
        for i in range(1, 8):
            p, to = member(i)
            out_copies[st, a].append(remote(
                out_buf.at[a, st, p // 2, pl.ds(pl.multiple_of((p % 2) * 128, 128), 128)], spot,
                s_out.at[st, a, i - 1], r_out.at[st, a, i - 1], to))
        copy = pltpu.make_async_copy(
            out_buf.at[a, st, x, pl.ds(pl.multiple_of(zb * 128, 128), 128)], spot,
            s_outl.at[st, a])
        copy.start()
        own_out[st, a] = copy

    def grads(st):
        sent[st, "dm"].wait_recv()
        sent[st, "sum"].wait_recv()
        mixeds, dsums, deltas = [], [], []
        for j in range(2):
            dms, summary = totals(st, j)
            inv = inv_save[2 * st + j]
            inv_t = split(inv.T)
            mixed = jnp.dot(
                inv, summary, precision=lax.Precision.HIGHEST, preferred_element_type=F32)
            dsum = dot(jnp.concatenate([inv_t[0], inv_t[1]], axis=1),
                       jnp.concatenate([dms, dms], axis=0))
            mixeds.append(mixed.astype(BF))
            dsums.append(dsum.astype(BF))
            deltas.append(jnp.sum((dsum * summary).T, axis=0, keepdims=True))
        for j in range(2):
            cut = slice(128 * j, 128 * j + 128)
            d_v = rounded(dot(rt[st, j], dsums[j])).reshape(RUNS, RUN, HD)
            out_buf[2, st, :, :, cut] = (out_buf[2, st, :, :, cut].astype(F32) + d_v).astype(BF)
        send_out(st, 2)
        for j in range(2):
            cut = slice(128 * j, 128 * j + 128)
            d_right = rounded(dot(head(st, 2, j), dsums[j], 1, 1))
            d_right = (rf[st, j] * (d_right - deltas[j]) * SCALE).astype(BF)
            d_k = dot(d_right, marks[0, 2 * st + j]).astype(BF)
            out_buf[1, st, :, :, cut] = d_k.reshape(RUNS, RUN, HD)
            dkq[st, 0, :, j] = dot(d_right, head(st, 1, j), 0, 0).astype(BF).reshape(
                2, LM // 2, HD)
        for j in range(2):
            cut = slice(128 * j, 128 * j + 128)
            left = lf[st, j]
            d_left = rounded(dot(mixeds[j], head(st, 3, j), 1, 1))
            prod = left * d_left
            d_left = ((prod - left * jnp.sum(prod, axis=0, keepdims=True)) * SCALE).astype(BF)
            d_q = dot(d_left, marks[1, 2 * st + j], 0, 0).astype(BF)
            out_buf[0, st, :, :, cut] = d_q.reshape(RUNS, RUN, HD)
            dkq[st, 1, :, j] = dot(d_left, head(st, 0, j)).astype(BF).reshape(2, LM // 2, HD)
        sent[st, "dkq"] = remote(
            dkq.at[st, :, other], dkq_in.at[st], s_dkq.at[st], r_dkq.at[st], partner)

    def reverse(st):
        chain = []
        for j in range(2):
            dms, summary = totals(st, j)
            s_t = split(summary.T)
            grad = dot(
                jnp.concatenate([dms, dms], axis=1), jnp.concatenate([s_t[0], s_t[1]], axis=0))
            chain.append([grad, jnp.zeros((LM, LM), F32), split(m_save[2 * st + j].T)])
        for it in reversed(range(ITERS)):
            for j in range(2):
                h = 2 * st + j
                grad, d_mid, m_t = chain[j]
                xt = (xt_save[h, it, 0], xt_save[h, it, 1])
                ps = (p_save[h, it, 0], p_save[h, it, 1])
                p2s = (p2_save[h, it, 0], p2_save[h, it, 1])
                js = (j_save[h, it, 0], j_save[h, it, 1])
                ws = split(grad)
                g_mat = 0.25 * mm3(xt, ws)
                gs = split(g_mat)
                u_mat = 7.0 * g_mat - mm3(gs, ps)
                us = split(u_mat)
                d_p = mm3(us, ps) + mm3(ps, us) - mm3(p2s, gs) - 15.0 * g_mat
                dps = split(d_p)
                d_mid = d_mid + mm3(dps, xt)
                grad = 0.25 * mm3(ws, js) + mm3(m_t, dps)
                chain[j] = [grad, d_mid, m_t]
        for j in range(2):
            h = 2 * st + j
            grad, d_mid, m_t = chain[j]
            middle = m_save[h]
            d_mid = d_mid + al_save[h, 0:1, :] * grad.T
            d_log = middle * (d_mid - jnp.sum(middle * d_mid, axis=1, keepdims=True)) * SCALE
            d_log = d_log.astype(BF)
            mid_grad[st, 0, j] = dot(d_log, marks[1, h]).reshape(2, LM // 2, HD)
            mid_grad[st, 1, j] = dot(d_log, marks[0, h], 0, 0).reshape(2, LM // 2, HD)

    def send_marks(st):
        sent[st, "dkq"].wait_recv()
        for j in range(2):
            cut = slice(128 * j, 128 * j + 128)
            both = []
            for n in range(2):
                rest = rounded(dkq[st, n, za, j].astype(F32) + dkq_in[st, n, j].astype(F32))
                rest = rounded(rest + rounded(mid_grad[st, n, j, za])) * (1.0 / SEG)
                both.append(rest.reshape(8, 8, HD))
            lg_out[st, :, :, cut] = jnp.concatenate(both, axis=1).astype(BF)
        lg_copies[st] = []
        spot = pl.ds(pl.multiple_of(group * 512 + st * 256, 256), 256)
        for i in range(1, 8):
            p, to = member(i)
            lg_copies[st].append(remote(
                lg_out.at[st, p], lg_in.at[:, spot], s_tg.at[st, i - 1], r_tg.at[st, i - 1], to))
        own = pltpu.make_async_copy(lg_out.at[st, group], lg_in.at[:, spot], s_lgl.at[st])
        own.start()
        own_out[st, 3] = own

    prepare(0)
    sum_up(0)
    issue(1, 3)
    issue(1, 2)
    prepare(1)
    convolve(0)
    grads(0)
    sum_up(1)
    convolve(1)
    taps_grad(0)
    taps_grad(1)
    dw_start()
    send_out(0, 1)
    send_out(0, 0)
    reverse(0)
    grads(1)
    send_out(1, 1)
    send_out(1, 0)
    send_marks(0)
    reverse(1)
    send_marks(1)
    dw_step(0)
    dw_step(1)
    dw_step(2)
    for st in range(NST):
        finish(st)
    dw_step(3)
    for copy in pending:
        copy.wait_send()


def add_marks(dq, dk, dv, marks_grad, dw, dq_out, dk_out, dv_out, dw_out):
    at = (pl.program_id(0) * ROWS + lax.broadcasted_iota(jnp.int32, (ROWS, 16), 0)) // SEG
    col = lax.broadcasted_iota(jnp.int32, (ROWS, 16), 1)
    for n, (part, out) in enumerate(((dq, dq_out), (dk, dk_out))):
        pick = jnp.where(col == at + 8 * n, 1.0, 0.0).astype(BF)
        out[0] = (part[0].astype(F32) + dot(pick, marks_grad[...])).astype(BF)
    dv_out[...] = dv[...]
    dw_out[...] = dw[0:2, 0:KW]


def shards(queries, key_vectors, value_vectors, cotangent, conv_weight):
    any_spec = pl.BlockSpec(memory_space=pl.ANY)
    vmem_spec = pl.BlockSpec(memory_space=pltpu.VMEM)
    full = jax.ShapeDtypeStruct(queries.shape, BF)
    dma = pltpu.SemaphoreType.DMA
    square = (LM, HD)
    chain = (4, ITERS, 2) + square
    dq, dk, dv, marks_grad, dw = pl.pallas_call(
        kernel,
        out_shape=(
            full, full, full, jax.ShapeDtypeStruct((16, full.shape[2]), BF),
            jax.ShapeDtypeStruct((8, 128), F32)),
        in_specs=[any_spec] * 4 + [vmem_spec],
        out_specs=(any_spec,) * 4 + (vmem_spec,),
        scratch_shapes=[
            pltpu.VMEM((2, 128, 4096), BF),
            pltpu.VMEM((16, 4096), BF),
            pltpu.VMEM((2, 8, 16, 512), BF),
            pltpu.VMEM((2, 4) + square, BF),
            pltpu.VMEM((4, 8, 128), F32),
            pltpu.VMEM((4, 2, RUN, EXT), BF),
            pltpu.VMEM((4, NST, RUNS, RUN, 256), BF),
            pltpu.VMEM((NST, 2, RUNS, 16, 256), BF),
            pltpu.VMEM((NST, 2, 16, 256), BF),
            pltpu.VMEM((NST, 2, 16, 256), BF),
            pltpu.VMEM((NST, 2, RUNS * RUN, LM), F32),
            pltpu.VMEM((NST, 2, RUNS * RUN, LM), BF),
            pltpu.VMEM((NST, 2, LM, RUNS * RUN), F32),
            pltpu.VMEM((NST, 2, 8, 128), F32),
            pltpu.VMEM((NST, 2, 2) + square, F32),
            pltpu.VMEM((NST, 2, 2) + square, BF),
            pltpu.VMEM((NST, 2, 2) + square, BF),
            pltpu.VMEM((4,) + square, F32),
            pltpu.VMEM((4,) + square, F32),
            pltpu.VMEM(chain, BF),
            pltpu.VMEM(chain, BF),
            pltpu.VMEM(chain, BF),
            pltpu.VMEM(chain, BF),
            pltpu.VMEM((4, 8, 128), F32),
            pltpu.VMEM((NST, 2, 2, 2, LM // 2, HD), BF),
            pltpu.VMEM((NST, 2, 2, LM // 2, HD), BF),
            pltpu.VMEM((NST, 2, 2, 2, LM // 2, HD), F32),
            pltpu.VMEM((NST, 8, 16, 256), BF),
            pltpu.VMEM((3, NST, RUNS, RUN, 256), BF),
            pltpu.VMEM((9, 8, 128), F32),
            pltpu.VMEM((7, 8, 128), F32),
            dma((3,)), dma((7,)), dma((7,)), dma, dma,
            dma((NST, 4, 7)), dma((NST, 4, 7)), dma((NST, 4)),
            dma((3,)), dma((3,)), dma((NST,)), dma((NST,)),
            dma((NST, 2)), dma((NST, 2)), dma((NST,)), dma((NST,)),
            dma((NST,)), dma((NST,)), dma((NST, 7)), dma((NST, 7)),
            dma((NST, 3, 7)), dma((NST, 3, 7)), dma((NST, 3)), dma((NST,)),
            dma((7,)), dma((7,)), dma((3,)), dma((3,)),
        ],
        compiler_params=pltpu.CompilerParams(
            collective_id=0, has_side_effects=True, vmem_limit_bytes=50 * 2**20
        ),
        cost_estimate=pl.CostEstimate(flops=2 * 10**9, bytes_accessed=7 * 2**20, transcendentals=0),
    )(queries, key_vectors, value_vectors, cotangent, conv_weight)
    block = pl.BlockSpec((1, ROWS, full.shape[2]), lambda i: (0, i, 0))

    def whole(shape):
        return pl.BlockSpec(shape, lambda i: (0, 0))

    return pl.pallas_call(
        add_marks,
        grid=(full.shape[1] // ROWS,),
        out_shape=(full, full, full, jax.ShapeDtypeStruct(conv_weight.shape, F32)),
        in_specs=[block] * 3 + [whole(marks_grad.shape), whole(dw.shape)],
        out_specs=(block, block, block, whole(conv_weight.shape)),
        compiler_params=pltpu.CompilerParams(vmem_limit_bytes=30 * 2**20),
    )(dq, dk, dv, marks_grad, dw)


def solution(mesh):
    return jax.shard_map(
        shards,
        mesh=mesh,
        in_specs=(
            P("dp", "seq", None),
            P("dp", "seq", None),
            P("dp", "seq", None),
            P("dp", "seq", None),
            P("seq", None),
        ),
        out_specs=(
            P("dp", "seq", None),
            P("dp", "seq", None),
            P("dp", "seq", None),
            P("seq", None),
        ),
        check_vma=False,
    )
```
